128 devices in a mesh: req: 4 (over y), exp: 32 (over z, x, core).
Axes of the slice: x: 4, y: 4, z: 4, core: 2. Of those that a mesh axis runs over, the one named last changes fastest.
Arguments:
- cand_emb: bfloat16 [32768, 1024], P(('req', 'exp')), may hold values from -6 to 6
- cand_request: int32 [32768], P(('req', 'exp')), may hold values from 0 to 1
- hist_blocks: int32 [256], P(('req', 'exp')), may hold values from 1 to 4
- cache_kv: bfloat16 [1024, 128, 2048], P(('req', 'exp')), may hold values from -20 to 20
- block_map: int32 [1024], P(('req', 'exp')), may hold values from 0 to 3, as said below
- w_query_update: bfloat16 [1024, 2048], replicated, may hold values from -0.1875 to 0.1875
- rel_bias: float32 [8, 4], replicated, may hold values from -4 to 4
- norm_gain: float32 [1024], replicated, may hold values from 0.5 to 1.5
- w_gate: bfloat16 [1024, 192], replicated, may hold values from -0.1875 to 0.1875
- expert_ids: int32 [32768, 2], P(('req', 'exp')), may hold values from 0 to 31, all different within a row; in each aligned block of 256 rows (0 to 255, 256 to 511, ...) at most 32 rows name the same one
- w_up: bfloat16 [32, 1024, 4096], P('exp'), may hold values from -0.1875 to 0.1875
- w_down: bfloat16 [32, 4096, 1024], P('exp'), may hold values from -0.09375 to 0.09375
- w_tower: bfloat16 [1024, 6], replicated, may hold values from -0.1875 to 0.1875
Outputs:
- task_scores: float32 [32768, 6], P(('req', 'exp'))
The draws below stay inside these ranges and needn't reach their ends.
Inputs may be any that keep to these rules, and one draw needn't show every extreme that they name: `block_map`: for each request, every block number from 0 to 3 is held by exactly one slot, and each owner holds 1 of them. `expert_ids`: among the candidates of one device no expert is chosen more than 32 times.
All inputs are finite; a program needn't handle non-finite values.
Results may differ from the reference program's by a relative error of at most 0.015.
Values may be sent and summed in bfloat16 or wider, within the bound.
No kernel may reach another device: no remote copies, remote signals or barrier semaphores. Data moves between devices by JAX's collectives and lax.ppermute only.
A program may use at most 128 MiB of HBM per device.

```python
import math
import jax
import jax.numpy as jnp
import numpy as np
from jax import lax

D = 1024
HEADS = 8
FF = 4096
TASKS = 6
EXPERTS = 32
TOP = 2
CAND_DEV = 256
REQ_DEV = 2
HB = 4
BLK = 128
G = 1
SLOTS = 8
CAP = 32
CANDS = 32768
REQUESTS = 256
N_REQ = 4
N_EXP = 32


def draw_cache_kv(key, part):
    key = jax.random.fold_in(key, 11)
    key_base, key_cols = jax.random.split(key, 2)
    slot_total = N_REQ * N_EXP * SLOTS
    entries = jax.random.truncated_normal(key_base, -4.0, 4.0, (slot_total, BLK, 2 * D), jnp.float32)
    spread = jnp.exp(jax.random.uniform(key_cols, (D,), jnp.float32, jnp.log(0.3), jnp.log(3.0)))
    column = jnp.concatenate([jnp.ones((D,), jnp.float32), spread])
    return (entries * column).astype(jnp.bfloat16)


def draw_block_map(key, part):
    key = jax.random.fold_in(key, 23)
    ordering = jnp.broadcast_to(jnp.arange(HB, dtype=jnp.int32), (N_REQ, N_EXP, REQ_DEV, HB))
    shuffled = jax.random.permutation(key, ordering, axis=3, independent=True)
    shuffled = shuffled.reshape(N_REQ, N_EXP, REQ_DEV, N_REQ, G)
    shuffled = jnp.transpose(shuffled, (3, 1, 0, 2, 4))
    return shuffled.reshape(-1).astype(jnp.int32)


def plant(drawn, rng, smallest, top_value):
    index_at = [jax.random.randint(jax.random.fold_in(rng, axis), (), 0, length) for axis, length in enumerate(drawn.shape)]
    main_axis = drawn.shape.index(max(drawn.shape))
    beside = index_at[:main_axis] + [(index_at[main_axis] + 1) % drawn.shape[main_axis]] + index_at[main_axis + 1:]
    return drawn.at[tuple(index_at)].set(smallest).at[tuple(beside)].set(top_value)


def block_levels(key, dims, pieces, least, largest):
    gain = 1.0
    for dim, blocks in pieces:
        draws = jax.random.uniform(jax.random.fold_in(jax.random.fold_in(key, 6), dim), (blocks,), jnp.float32, least / len(pieces), largest / len(pieces))
        gain = gain * jnp.repeat(jnp.exp(draws), dims[dim] // blocks).reshape((-1,) + (1,) * (len(dims) - 1 - dim))
    return gain


def deal_out(stream_key, own, number, rows, number_of, top, most, slope):
    ranking = jax.random.permutation(stream_key, number_of)
    crowded, usual = load_shares(number_of, rows * top, most, slope, True), load_shares(number_of, rows * top, most, slope, False)
    places = jnp.arange(number_of)

    def named(tallies, offset_by):
        used = int((tallies > 0).sum())
        fixed = max(1, used // 4)
        shifted = fixed + (places - fixed + offset_by * (used - fixed)) % max(1, number_of - fixed)
        return jnp.zeros((number_of,), jnp.int32).at[ranking[jnp.where(places < fixed, places, shifted)]].set(jnp.asarray(tallies, jnp.int32))

    tallies = jnp.where(number % 4 == 0, named(crowded, number // 4), named(usual, number - number // 4 - 1))
    mixed = jax.random.permutation(jax.random.fold_in(own, 3), number_of)
    donor, taker = mixed[0:number_of // 2 * 2:2], mixed[1:number_of // 2 * 2:2]
    margin = jnp.minimum(tallies[donor] - 1, most - tallies[taker]) // 2
    margin = jnp.where((donor == ranking[0]) | (taker == ranking[0]) | (tallies[taker] == 0), 0, jnp.maximum(margin, 0))
    shifted = jax.random.randint(jax.random.fold_in(own, 4), (number_of // 2,), 0, 1 << 20) % (margin + 1)
    tallies = tallies.at[donor].add(-shifted).at[taker].add(shifted)
    items = jnp.searchsorted(jnp.cumsum(tallies), jnp.arange(rows * top), side="right").astype(jnp.int32)
    listing = items.reshape(top, rows).T
    listing = listing[jax.random.permutation(jax.random.fold_in(own, 1), rows)]
    offset_by = jax.random.randint(jax.random.fold_in(own, 2), (rows, 1), 0, top)
    return jnp.take_along_axis(listing, (jnp.arange(top)[None, :] + offset_by) % top, axis=1)


def load_shares(count, total, most, slope, full):
    portions = [(1 << 20) // math.isqrt(rank ** slope) + 1 for rank in range(1, count + 1)]
    largest = most if full else min(most, max(-(-total // count), total * portions[0] // sum(portions)))
    least = 1 if total - largest >= count - 1 else 0
    holding, rest = [largest] + [least] * (count - 1), total - largest - least * (count - 1)
    while rest > 0:
        candidates = [i for i in range(1, count) if holding[i] < largest] or [i for i in range(1, count) if holding[i] < most]
        mass, budget = sum([portions[i] for i in candidates]), rest
        for i in candidates:
            more = min(most - holding[i], max(1, budget * portions[i] // mass), rest)
            holding[i] = holding[i] + more
            rest = rest - more
    return np.array(holding)


def scatter_about(own_key, dims, deviation, limit, shards=(), held_as=jnp.bfloat16):
    loudness = block_levels(own_key, dims, shards, -0.22, 0.18) if shards else 1.0
    drawn = jax.random.normal(own_key, dims, jnp.float32) * deviation * loudness
    return jnp.minimum(jnp.maximum(drawn, -limit), limit).astype(held_as)


def setup_inputs(seed: int = 0) -> dict:
    arg_keys = jax.random.split(jax.random.key(seed), 14)
    cand_emb = scatter_about(arg_keys[0], (CANDS, D), 1.0, 6.0, ((0, 128),))
    cand_request = plant(jax.random.randint(arg_keys[1], (CANDS,), 0, REQ_DEV), jax.random.fold_in(arg_keys[1], 1), 0, REQ_DEV - 1).astype(jnp.int32)
    hist_blocks = plant(jax.random.randint(arg_keys[2], (REQUESTS,), 1, HB + 1), jax.random.fold_in(arg_keys[2], 1), 1, HB).astype(jnp.int32)
    cache_kv = draw_cache_kv(jax.random.fold_in(arg_keys[13], 71), 0)
    block_map = draw_block_map(jax.random.fold_in(arg_keys[13], 71), 0)
    w_query_update = scatter_about(arg_keys[5], (D, 2 * D), D ** -0.5, 0.1875)
    rel_bias = scatter_about(arg_keys[6], (HEADS, HB), 1.0, 4.0, (), jnp.float32)
    norm_gain = jnp.clip(jax.random.uniform(arg_keys[7], (D,), jnp.float32, 0.5, 1.5), 0.5, 1.5)
    w_gate = scatter_about(arg_keys[8], (D, TASKS * EXPERTS), D ** -0.5, 0.1875)
    expert_ids_keys = jax.random.split(jax.random.fold_in(arg_keys[9], 1), CANDS // CAND_DEV)
    expert_ids_turns = jax.random.permutation(jax.random.fold_in(arg_keys[9], 3), CANDS // CAND_DEV)
    expert_ids = jax.vmap(lambda own, number: deal_out(jax.random.fold_in(arg_keys[9], 2), own, number, CAND_DEV, EXPERTS, TOP, CAP, 2))(expert_ids_keys, expert_ids_turns).reshape((CANDS, TOP))
    w_up = scatter_about(arg_keys[10], (EXPERTS, D, FF), D ** -0.5, 0.1875, ((0, 32),))
    w_down = scatter_about(arg_keys[11], (EXPERTS, FF, D), FF ** -0.5, 0.09375, ((0, 32),))
    w_tower = scatter_about(arg_keys[12], (D, TASKS), D ** -0.5, 0.1875)
    return {"cand_emb": cand_emb, "cand_request": cand_request, "hist_blocks": hist_blocks, "cache_kv": cache_kv, "block_map": block_map, "w_query_update": w_query_update, "rel_bias": rel_bias, "norm_gain": norm_gain, "w_gate": w_gate, "expert_ids": expert_ids, "w_up": w_up, "w_down": w_down, "w_tower": w_tower}


EPSILON = 1e-05

def attend(queries, keys_values, key_group, key_block, cand_group, group_blocks, rel_bias):
    row_count, feature = queries.shape
    head_count = rel_bias.shape[0]
    head_dim = feature // head_count
    key_part = keys_values[:, :feature].reshape(-1, head_count, head_dim).astype(jnp.float32)
    value_part = keys_values[:, feature:].reshape(-1, head_count, head_dim).astype(jnp.float32)
    query_heads = queries.reshape(row_count, head_count, head_dim).astype(jnp.float32)
    scores = jnp.einsum('chd,nhd->hcn', query_heads, key_part)
    block_hot = (key_block[:, None] == jnp.arange(rel_bias.shape[1], dtype=jnp.int32)[None, :]).astype(jnp.float32)
    block_bias = lax.optimization_barrier(jnp.sum(rel_bias[:, None, :] * block_hot[None, :, :], axis=2))
    scores = scores * (1.0 / math.sqrt(head_dim)) + block_bias[:, None, :]
    group_hot = cand_group[:, None] == jnp.arange(group_blocks.shape[0], dtype=jnp.int32)[None, :]
    group_len = lax.optimization_barrier(jnp.sum(jnp.where(group_hot, group_blocks[None, :], 0), axis=1))
    allowed = (cand_group[:, None] == key_group[None, :]) & (key_block[None, :] < group_len[:, None])
    weights = jnp.where(allowed[None], jax.nn.silu(scores), 0.0).astype(jnp.bfloat16)
    attended = jnp.einsum('hcn,nhd->chd', weights.astype(jnp.float32), value_part)
    return attended.reshape(row_count, feature)

def token_mixer(cand_rows, cand_map, group_blocks, keys_values, key_group, key_block, w_query_update, rel_bias, norm_gain):
    feature = cand_rows.shape[1]
    projected = jnp.dot(cand_rows, w_query_update, preferred_element_type=jnp.float32)
    queries = projected[:, :feature].astype(jnp.bfloat16)
    update = jax.nn.silu(projected[:, feature:])
    owner_keys = keys_values.shape[0] // N_REQ
    attended = jnp.zeros((cand_rows.shape[0], feature), jnp.float32)
    for owner in range(N_REQ):
        first = owner * owner_keys
        partial_value = attend(queries, keys_values[first:first + owner_keys], key_group[first:first + owner_keys], key_block[first:first + owner_keys], cand_map, group_blocks, rel_bias)
        rounded = lax.optimization_barrier(partial_value.astype(jnp.bfloat16))
        attended = attended + rounded.astype(jnp.float32)
    inv_rms = lax.rsqrt(lax.optimization_barrier(jnp.mean(attended * attended, axis=1, keepdims=True)) + EPSILON)
    return (cand_rows.astype(jnp.float32) + norm_gain * attended * inv_rms * update).astype(jnp.bfloat16)

def reference(cand_emb, cand_request, hist_blocks, cache_kv, block_map, w_query_update, rel_bias, norm_gain, w_gate, expert_ids, w_up, w_down, w_tower):
    device_total = N_REQ * N_EXP
    group_slots = REQ_DEV * G
    cache_view = cache_kv.reshape(N_REQ, N_EXP, N_REQ, group_slots, BLK, 2 * D)
    block_view = block_map.reshape(N_REQ, N_EXP, N_REQ, group_slots)
    slot_index = jnp.arange(N_REQ * group_slots, dtype=jnp.int32)
    key_group = jnp.repeat(slot_index // G % REQ_DEV, BLK)

    def one_device(device):
        device_row = device // N_EXP
        device_col = device % N_EXP
        keys_values = cache_view[:, device_col, device_row].reshape(N_REQ * group_slots * BLK, 2 * D)
        key_block = jnp.repeat(block_view[:, device_col, device_row].reshape(-1), BLK)
        cand_rows = lax.dynamic_slice_in_dim(cand_emb, device * CAND_DEV, CAND_DEV, 0)
        cand_map = lax.dynamic_slice_in_dim(cand_request, device * CAND_DEV, CAND_DEV, 0)
        group_blocks = lax.dynamic_slice_in_dim(hist_blocks, device * REQ_DEV, REQ_DEV, 0)
        return token_mixer(cand_rows, cand_map, group_blocks, keys_values, key_group, key_block, w_query_update, rel_bias, norm_gain)
    mixed_rows = lax.map(one_device, jnp.arange(device_total, dtype=jnp.int32)).reshape(CANDS, D)
    logits = jnp.dot(mixed_rows, w_gate, preferred_element_type=jnp.float32).reshape(CANDS, TASKS, EXPERTS)
    expert_range = jnp.arange(EXPERTS, dtype=jnp.int32)
    chosen = (expert_ids[:, :, None] == expert_range[None, None, :]).astype(jnp.float32)
    picked = lax.optimization_barrier(jnp.sum(logits[:, :, None, :] * chosen[:, None, :, :], axis=3))
    squashed = jax.nn.sigmoid(picked)
    gates = squashed / lax.optimization_barrier(jnp.sum(squashed, axis=2, keepdims=True))
    flat_ids = expert_ids.reshape(device_total, CAND_DEV * TOP)
    route_hot = (flat_ids[:, :, None] == expert_range[None, None, :]).astype(jnp.int32)
    position = lax.optimization_barrier(jnp.sum(jnp.cumsum(route_hot, axis=1) * route_hot, axis=2)) - 1
    device_ids = jnp.arange(device_total, dtype=jnp.int32)[:, None]
    slot_global = ((flat_ids * device_total + device_ids) * CAP + position).reshape(-1)
    source = jnp.zeros((EXPERTS * device_total * CAP,), jnp.int32).at[slot_global].set(jnp.arange(CANDS * TOP, dtype=jnp.int32) + 1)

    def run_expert(operands):
        sources, up_matrix, down_matrix = operands
        filled = sources > 0
        rows_in = jnp.where(filled[:, None], mixed_rows[jnp.maximum(sources - 1, 0) // TOP], jnp.zeros((), jnp.bfloat16))
        hidden = jax.nn.silu(jnp.dot(rows_in, up_matrix, preferred_element_type=jnp.float32)).astype(jnp.bfloat16)
        produced = jnp.dot(hidden, down_matrix, preferred_element_type=jnp.float32).astype(jnp.bfloat16)
        return jnp.dot(produced, w_tower, preferred_element_type=jnp.float32)
    projected = lax.map(run_expert, (source.reshape(EXPERTS, device_total * CAP), w_up, w_down)).reshape(-1, TASKS)
    per_route = projected[slot_global].reshape(CANDS, TOP, TASKS)
    return lax.optimization_barrier(jnp.sum(gates * jnp.transpose(per_route, (0, 2, 1)), axis=2))
```

```python
import functools
import math

import jax
import jax.numpy as jnp
from jax import lax
from jax.experimental import pallas as pl
from jax.experimental.pallas import tpu as pltpu
from jax.sharding import PartitionSpec as P

EPSILON = 1e-05
F32 = jnp.float32
BF16 = jnp.bfloat16
NT = (((1,), (1,)), ((), ()))


def attend_kernel(
    heads_step,
    block_ref,
    hist_ref,
    bias_ref,
    req_ref,
    query_ref,
    k0,
    v0,
    k1,
    v1,
    k2,
    v2,
    k3,
    v3,
    cand_ref,
    update_ref,
    gain_ref,
    place_ref,
    out_ref,
    mixed_ref,
    attended,
):
    step = pl.program_id(0)
    rows = req_ref.shape[0]
    first = jnp.broadcast_to(req_ref[...], (rows, 128)) == 0
    for part in range(heads_step):
        head = step * heads_step + part
        cols = pl.ds(part * 128, 128)
        query = query_ref[:, cols]
        total = None
        for owner, (key_ref, value_ref) in enumerate(((k0, v0), (k1, v1), (k2, v2), (k3, v3))):
            scores = lax.dot_general(query, key_ref[:, cols], NT, preferred_element_type=F32)
            scores = jnp.where(first, scores[:, :128], scores[:, 128:])
            block_a = block_ref[owner, 0]
            block_b = block_ref[owner, 1]
            bias = jnp.where(first, bias_ref[head, block_a], bias_ref[head, block_b])
            half = (scores * (1.0 / math.sqrt(128.0)) + bias) * 0.5
            weight = half + half * jnp.tanh(half)
            live_a = jnp.where(block_a < hist_ref[0], 1.0, 0.0)
            live_b = jnp.where(block_b < hist_ref[1], 1.0, 0.0)
            weight_a = jnp.where(first, weight * live_a, 0.0)
            weight_b = jnp.where(first, 0.0, weight * live_b)
            weights = jnp.concatenate([weight_a, weight_b], axis=1).astype(BF16)
            partial = jnp.dot(weights, value_ref[:, cols], preferred_element_type=F32)
            total = partial if total is None else total + partial
        attended[step, :, cols] = total

    @pl.when(step == pl.num_programs(0) - 1)
    def _():
        steps = attended.shape[0]
        width = attended.shape[2]
        square = None
        for i in range(steps):
            item = attended[i]
            item = jnp.sum(item * item, axis=1, keepdims=True)
            square = item if square is None else square + item
        inv_rms = lax.rsqrt(square * (1.0 / (steps * width)) + EPSILON)
        for i in range(steps):
            cols = pl.ds(i * width, width)
            mixed = cand_ref[:, cols].astype(F32) + gain_ref[:, cols] * attended[i] * inv_rms * update_ref[:, cols]
            mixed = mixed.astype(BF16)
            mixed_ref[:, cols] = mixed
            out_ref[:, cols] = jnp.dot(place_ref[...], mixed, preferred_element_type=F32).astype(BF16)


def expert_kernel(row_tile, x_ref, up_ref, tower_ref, out_ref, total):
    step = pl.program_id(0)
    rows = x_ref.shape[0]

    @pl.when(step == 0)
    def _():
        total[...] = jnp.zeros_like(total)

    for start in range(0, rows, row_tile):
        at = pl.ds(start, row_tile)
        half = jnp.dot(x_ref[at, :], up_ref[...], preferred_element_type=F32) * 0.5
        hidden = (half + half * jnp.tanh(half)).astype(BF16)
        total[at, :] += jnp.dot(hidden, tower_ref[...], preferred_element_type=F32)

    @pl.when(step == pl.num_programs(0) - 1)
    def _():
        peers = out_ref.shape[0]
        share = rows // peers
        zero = jnp.zeros((8, 128 - share), F32)
        for tile in range(rows // 128):
            turned = jnp.transpose(total[pl.ds(tile * 128, 128), :])
            turned = turned[0:8, :] + turned[8:16, :]
            for i in range(128 // share):
                piece = turned[:, i * share : (i + 1) * share]
                out_ref[tile * (128 // share) + i] = jnp.concatenate([piece, zero], axis=1)


def combine_kernel(slot_ref, weight_ref, back_ref, out_ref):
    routes = slot_ref.shape[0]
    rows = routes // 2
    hot = slot_ref[...]
    back = back_ref[...]
    high = back.astype(BF16)
    rest = back - high.astype(F32)
    middle = rest.astype(BF16)
    low = (rest - middle.astype(F32)).astype(BF16)
    found = lax.dot_general(hot, high, NT, preferred_element_type=F32)
    found += lax.dot_general(hot, middle, NT, preferred_element_type=F32)
    found += lax.dot_general(hot, low, NT, preferred_element_type=F32)
    found = found * weight_ref[...]
    found = found[:rows] + found[rows:]
    found = found[:, :128] + found[:, 128:]
    for shift in (64, 32, 16, 8):
        found = found + pltpu.roll(found, shift, 1)
    out_ref[...] = found[:, : out_ref.shape[1]]


def local(
    cand_emb,
    cand_request,
    hist_blocks,
    cache_kv,
    block_map,
    w_query_update,
    rel_bias,
    norm_gain,
    w_gate,
    expert_ids,
    w_up,
    w_down,
    w_tower,
):
    rows, feature = cand_emb.shape
    owners = lax.axis_size("req")
    me = lax.axis_index("req")
    task_count = w_tower.shape[1]
    expert_count = w_gate.shape[1] // task_count
    top_count = expert_ids.shape[1]
    capacity = 2 * rows * top_count // expert_count
    slots = expert_count * capacity

    cache = cache_kv.reshape(owners, -1, 2 * feature)
    ids = block_map.reshape(owners, 1, -1)
    moved = [lax.dynamic_index_in_dim(cache, me, 0, False)]
    moved_ids = [lax.dynamic_index_in_dim(ids, me, 0, False)]
    for shift in (1, 3, 2):
        to = lax.rem(me + shift, owners)
        pairs = [(i, (i + shift) % owners) for i in range(owners)]
        moved_ids.append(lax.ppermute(lax.dynamic_index_in_dim(ids, to, 0, False), "req", pairs))
        moved.append(lax.ppermute(lax.dynamic_index_in_dim(cache, to, 0, False), "req", pairs))
    blocks = jnp.concatenate(moved_ids, axis=0)

    projected = jnp.dot(cand_emb, w_query_update, preferred_element_type=F32)
    queries = projected[:, :feature].astype(BF16)
    update = jax.nn.silu(projected[:, feature:])

    tower = jnp.dot(w_down[0], w_tower, preferred_element_type=F32)
    tower_high = lax.reduce_precision(tower, 8, 7)
    tower_low = tower - tower_high
    gap = jnp.zeros((tower.shape[0], 8 - task_count), BF16)
    tower_parts = jnp.concatenate(
        [
            tower_high.astype(BF16),
            gap,
            tower_low.astype(BF16),
            gap,
            jnp.zeros((tower.shape[0], 112), BF16),
        ],
        axis=1,
    )

    expert_range = jnp.arange(expert_count, dtype=jnp.int32)
    hot = (expert_ids[:, :, None] == expert_range).astype(BF16)
    hot_both = jnp.concatenate([hot[:, 0], hot[:, 1]], axis=0)
    routes = hot_both.shape[0]
    earlier = jnp.tril(jnp.ones((routes, routes), BF16), -1)
    counts = jnp.dot(earlier, hot_both, preferred_element_type=F32)
    position = jnp.sum(counts * hot_both.astype(F32), axis=1).astype(jnp.int32)
    flat_ids = jnp.concatenate([expert_ids[:, 0], expert_ids[:, 1]], axis=0)
    slot_of = flat_ids * capacity + position
    slot_range = jnp.arange(slots, dtype=jnp.int32)[:, None]
    place = (
        (slot_of[None, :rows] == slot_range) | (slot_of[None, rows:] == slot_range)
    ).astype(BF16)
    slot_hot = (position[:, None] == jnp.arange(128, dtype=jnp.int32)[None, :]).astype(BF16)

    heads_step = 2
    width = heads_step * 128
    steps = feature // width
    keys = moved[0].shape[0]
    whole = lambda *shape: pl.BlockSpec(shape, lambda i, *_: (0,) * len(shape))
    smem = pl.BlockSpec(memory_space=pltpu.SMEM)
    kv_specs = []
    kv_args = []
    for item in moved:
        kv_specs.append(pl.BlockSpec((keys, width), lambda i: (0, i)))
        kv_specs.append(pl.BlockSpec((keys, width), lambda i: (0, i + steps)))
        kv_args += [item, item]
    outgoing, mixed_rows = pl.pallas_call(
        functools.partial(attend_kernel, heads_step),
        grid=(steps,),
        in_specs=[
            smem,
            smem,
            smem,
            whole(rows, 1),
            pl.BlockSpec((rows, width), lambda i: (0, i)),
            *kv_specs,
            whole(rows, feature),
            whole(rows, feature),
            whole(1, feature),
            whole(slots, rows),
        ],
        out_specs=[whole(slots, feature), whole(rows, feature)],
        out_shape=[
            jax.ShapeDtypeStruct((slots, feature), BF16),
            jax.ShapeDtypeStruct((rows, feature), BF16),
        ],
        scratch_shapes=[pltpu.VMEM((steps, rows, width), F32)],
        compiler_params=pltpu.CompilerParams(vmem_limit_bytes=40 * 2**20),
        cost_estimate=pl.CostEstimate(flops=2 * 10**9, bytes_accessed=9 * 10**6, transcendentals=2**20),
        name="attend",
    )(
        blocks,
        hist_blocks,
        rel_bias,
        cand_request[:, None],
        queries,
        *kv_args,
        cand_emb,
        update,
        norm_gain[None, :],
        place,
    )

    arrived = lax.all_to_all(
        outgoing.reshape(expert_count, capacity, feature), "exp", split_axis=0, concat_axis=0, tiled=True
    )

    logits = jnp.dot(mixed_rows, w_gate, preferred_element_type=F32).reshape(
        rows, 1, task_count, expert_count
    )
    picked = jnp.sum(logits * hot.astype(F32)[:, :, None, :], axis=3)
    squashed = jax.nn.sigmoid(picked)
    gates = squashed / jnp.sum(squashed, axis=1, keepdims=True)
    gates = jnp.pad(gates, ((0, 0), (0, 0), (0, 8 - task_count)))
    spread = hot.astype(F32)[:, :, :, None] * gates[:, :, None, :]
    spread = spread.reshape(rows, top_count, expert_count * 8)
    spread = jnp.concatenate([spread[:, 0], spread[:, 1]], axis=0)

    hidden_count = w_up.shape[2]
    tile = 512
    produced = pl.pallas_call(
        functools.partial(expert_kernel, 256),
        grid=(hidden_count // tile,),
        in_specs=[
            whole(slots, feature),
            pl.BlockSpec((feature, tile), lambda i: (0, i)),
            pl.BlockSpec((tile, 128), lambda i: (i, 0)),
        ],
        out_specs=whole(expert_count, 8, 128),
        out_shape=jax.ShapeDtypeStruct((expert_count, 8, 128), F32),
        scratch_shapes=[pltpu.VMEM((slots, 128), F32)],
        compiler_params=pltpu.CompilerParams(vmem_limit_bytes=40 * 2**20),
        cost_estimate=pl.CostEstimate(flops=11 * 10**9, bytes_accessed=11 * 10**6, transcendentals=2**22),
        name="expert",
    )(arrived.reshape(slots, feature), w_up[0], tower_parts)

    came_back = lax.all_to_all(produced, "exp", split_axis=0, concat_axis=0, tiled=True)

    return pl.pallas_call(
        combine_kernel,
        out_shape=jax.ShapeDtypeStruct((rows, task_count), F32),
        cost_estimate=pl.CostEstimate(flops=10**8, bytes_accessed=10**6, transcendentals=0),
        name="combine",
    )(slot_hot, spread, came_back.reshape(expert_count * 8, 128))


def solution(mesh):
    placed = (
        P(("req", "exp"), None),
        P(("req", "exp")),
        P(("req", "exp")),
        P(("req", "exp"), None, None),
        P(("req", "exp")),
        P(),
        P(),
        P(),
        P(),
        P(("req", "exp"), None),
        P("exp", None, None),
        P("exp", None, None),
        P(),
    )
    return jax.shard_map(
        local, mesh=mesh, in_specs=placed, out_specs=P(("req", "exp"), None), check_vma=False
    )
```

```python
import functools
import math

import jax
import jax.numpy as jnp
from jax import lax
from jax.experimental import pallas as pl
from jax.experimental.pallas import tpu as pltpu
from jax.sharding import PartitionSpec as P

EPSILON = 1e-05
F32 = jnp.float32
BF16 = jnp.bfloat16
NT = (((1,), (1,)), ((), ()))
TN = (((0,), (0,)), ((), ()))
SHIFTS = (1, 3, 2)
LIMIT = 63 * 2**20


def pack_kernel(me_ref, ids_ref, *refs):
    count = len(SHIFTS)
    ins, outs = refs[: 2 * count], refs[2 * count :]
    keys = ins[0].shape[1]
    heads = ins[0].shape[2] // 128
    for n, shift in enumerate(SHIFTS):
        for head in range(heads):
            cols = pl.ds(head * 128, 128)
            outs[n][pl.ds(head * keys, keys), :] = ins[2 * n][0, :, cols]
            outs[n][pl.ds((heads + head) * keys, keys), :] = ins[2 * n + 1][0, :, cols]
    if len(outs) > count:
        row = lax.broadcasted_iota(jnp.int32, (16, 128), 0)
        me = me_ref[0]

        def tile_of(owner):
            first = ids_ref[2 * owner].astype(F32)
            second = ids_ref[2 * owner + 1].astype(F32)
            return jnp.where(row == 0, first, second).astype(BF16)

        for n, shift in enumerate(SHIFTS):
            outs[n][pl.ds(2 * heads * keys, 16), :] = tile_of(lax.rem(me + shift, count + 1))
        outs[count][...] = tile_of(me)


def route_kernel(capacity, lane_ref, ids_ref, cand_ref, place_ref, slot_ref, out_ref):
    rows = ids_ref.shape[1]
    experts = place_ref.shape[0] // capacity
    ids = jnp.concatenate([ids_ref[0:1, :], ids_ref[1:2, :]], axis=1)
    hot = lax.broadcasted_iota(jnp.int32, (experts, 2 * rows), 0) == ids
    hot = jnp.where(hot, 1.0, 0.0)
    here = lax.broadcasted_iota(jnp.int32, (2 * rows, 2 * rows), 0)
    there = lax.broadcasted_iota(jnp.int32, (2 * rows, 2 * rows), 1)
    earlier = jnp.where(here < there, 1.0, 0.0).astype(BF16)
    counts = jnp.dot(hot.astype(BF16), earlier, preferred_element_type=F32)
    position = jnp.sum(counts * hot, axis=0, keepdims=True).astype(jnp.int32)
    slot = ids * capacity + position
    spot = lax.broadcasted_iota(jnp.int32, place_ref.shape, 0)
    place = (spot == slot[:, :rows]) | (spot == slot[:, rows:])
    place = jnp.where(place, 1.0, 0.0).astype(BF16)
    place_ref[...] = place
    lane = position + lane_ref[0]
    lanes = lax.broadcasted_iota(jnp.int32, slot_ref.shape, 0) == lane
    slot_ref[...] = jnp.where(lanes, 1.0, 0.0).astype(BF16)
    out_ref[...] = jnp.dot(place, cand_ref[...], preferred_element_type=F32).astype(BF16)


def project_kernel(feature, cand_ref, weight_ref, query_ref, update_ref):
    step = pl.program_id(0)
    half = pl.num_programs(0) // 2
    projected = jnp.dot(cand_ref[...], weight_ref[...], preferred_element_type=F32)

    @pl.when(step < half)
    def _():
        query_ref[...] = projected.astype(BF16)

    @pl.when(step >= half)
    def _():
        update_ref[...] = projected / (1.0 + jnp.exp(-projected))


def tower_kernel(down_ref, tower_ref, out_ref):
    product = lax.dot_general(tower_ref[...], down_ref[...], NT, preferred_element_type=F32)
    high = product.astype(BF16)
    low = (product - high.astype(F32)).astype(BF16)
    out_ref[...] = jnp.concatenate([high[0:8], low[0:8]], axis=0)


def attend_head(head, first, masks, query, parts, tiles, bias_ref):
    total = None
    for owner, (key, value) in enumerate(parts):
        scores = lax.dot_general(query, key, NT, preferred_element_type=F32)
        scores = jnp.where(first, scores[:, :128], scores[:, 128:])
        block_a, block_b = tiles[owner]
        bias_a = jnp.zeros_like(block_a)
        bias_b = jnp.zeros_like(block_b)
        for block in range(bias_ref.shape[1]):
            entry = bias_ref[head, block] * 0.5
            bias_a = jnp.where(block_a == block, entry, bias_a)
            bias_b = jnp.where(block_b == block, entry, bias_b)
        half = scores * (0.5 / math.sqrt(128.0)) + jnp.where(first, bias_a, bias_b)
        weight = (half + half * jnp.tanh(half)).astype(BF16)
        weight = jnp.concatenate([weight, weight], axis=1) * masks[owner]
        partial = jnp.dot(weight, value, preferred_element_type=F32)
        total = partial if total is None else total + partial
    return total


def block_rows(tile_refs):
    rows = []
    for ref in tile_refs:
        tile = ref[...].astype(F32)
        rows.append((tile[0:1, :], tile[1:2, :]))
    return rows


def fill_masks(first, tiles, hist_ref, masks):
    length_a = hist_ref[0].astype(F32)
    length_b = hist_ref[1].astype(F32)
    for owner, (block_a, block_b) in enumerate(tiles):
        live_a = jnp.where(block_a < length_a, 1.0, 0.0)
        live_b = jnp.where(block_b < length_b, 1.0, 0.0)
        mask_a = jnp.where(first, live_a, 0.0)
        mask_b = jnp.where(first, 0.0, live_b)
        masks[owner] = jnp.concatenate([mask_a, mask_b], axis=1).astype(BF16)


def attend_first_kernel(
    me_ref, hist_ref, bias_ref, req_ref, query_ref, k0, v0, k1, v1, k2, v2, k3, v3,
    t0, t1, t2, t3, update_ref, gain_ref, place_ref, out_ref, stuff_ref, square_ref, masks,
):
    head = pl.program_id(0)
    rows = req_ref.shape[0]
    first = jnp.broadcast_to(req_ref[...], (rows, 128)) == 0
    tiles = block_rows((t0, t1, t2, t3))

    @pl.when(head == 0)
    def _():
        fill_masks(first, tiles, hist_ref, masks)
        square_ref[...] = jnp.zeros_like(square_ref)

    parts = ((k0[0], v0[0]), (k1[...], v1[...]), (k2[...], v2[...]), (k3[...], v3[...]))
    attended = attend_head(head, first, masks, query_ref[...], parts, tiles, bias_ref)
    square_ref[...] += attended * attended
    stuff = (gain_ref[...] * attended * update_ref[...]).astype(BF16)
    stuff_ref[...] = stuff
    out_ref[...] = jnp.dot(place_ref[...], stuff, preferred_element_type=F32).astype(BF16)


def attend_last_kernel(
    me_ref, hist_ref, bias_ref, req_ref, query_ref, k0, v0, k1, v1, k2, v2, k3, v3,
    t0, t1, t2, t3, update_ref, gain_ref, place_ref, cand_ref, stuff_ref, square_ref,
    out_ref, mixed_ref, masks, attended,
):
    step = pl.program_id(0)
    heads = pl.num_programs(0)
    rows = req_ref.shape[0]
    first = jnp.broadcast_to(req_ref[...], (rows, 128)) == 0
    tiles = block_rows((t0, t1, t2, t3))

    @pl.when(step == 0)
    def _():
        fill_masks(first, tiles, hist_ref, masks)

    parts = ((k0[0], v0[0]), (k1[...], v1[...]), (k2[...], v2[...]), (k3[...], v3[...]))
    found = attend_head(step + heads, first, masks, query_ref[...], parts, tiles, bias_ref)
    attended[step] = found

    @pl.when(step == heads - 1)
    def _():
        count = attended.shape[0]
        feature = cand_ref.shape[1]
        early = feature - count * 128
        square = square_ref[...]
        for i in range(count):
            square = square + attended[i] * attended[i]
        mean = jnp.sum(square, axis=1, keepdims=True) * (1.0 / feature)
        inv_rms = lax.rsqrt(mean + EPSILON)
        mixed = cand_ref[:, :early].astype(F32) + stuff_ref[...].astype(F32) * inv_rms
        mixed_ref[:, :early] = mixed.astype(BF16)
        place = place_ref[...]
        peers = out_ref.shape[0]
        share = place.shape[0] // peers
        for i in range(count):
            cols = pl.ds(early + i * 128, 128)
            here = pl.ds(i * 128, 128)
            mixed = cand_ref[:, cols].astype(F32)
            mixed = mixed + gain_ref[:, here] * attended[i] * update_ref[:, here] * inv_rms
            mixed = mixed.astype(BF16)
            mixed_ref[:, cols] = mixed
            moved = jnp.dot(place, mixed, preferred_element_type=F32).astype(BF16)
            out_ref[:, pl.ds(i * share, share), :] = moved.reshape(peers, share, 128)
        lane = lax.broadcasted_iota(jnp.int32, (rows, 128), 1)
        high = inv_rms.astype(BF16).astype(F32)
        low = inv_rms - high
        scale = jnp.where(lane == 0, high, jnp.where(lane == 1, low, 0.0)).astype(BF16)
        moved = jnp.dot(place, scale, preferred_element_type=F32).reshape(peers, share, 128)
        early_part = moved[:, : share // 2, :]
        late_part = moved[:, share // 2 :, :].reshape(peers * share // 2, 128)
        late_part = pltpu.roll(late_part, 64, 1).reshape(peers, share // 2, 128)
        out_ref[:, pl.ds(count * share, share // 2), :] = (early_part + late_part).astype(BF16)


def gate_kernel(tasks, ids_ref, weight_ref, mixed_ref, out_ref):
    rows = mixed_ref.shape[0]
    experts = weight_ref.shape[0] // tasks
    logits = lax.dot_general(weight_ref[...], mixed_ref[...], NT, preferred_element_type=F32)
    squashed = []
    for k in range(2):
        hot = lax.broadcasted_iota(jnp.int32, (experts, rows), 0) == ids_ref[k : k + 1, :]
        picked = []
        for task in range(8):
            if task < tasks:
                here = logits[task * experts : (task + 1) * experts, :]
                picked.append(jnp.sum(jnp.where(hot, here, 0.0), axis=0, keepdims=True))
            else:
                picked.append(jnp.zeros((1, rows), F32))
        squashed.append(jax.nn.sigmoid(jnp.concatenate(picked, axis=0)))
    whole = squashed[0] + squashed[1]
    for k in range(2):
        gates = squashed[k] / whole
        ids = ids_ref[k : k + 1, :]
        for expert in range(experts):
            out_ref[pl.ds(expert * 8, 8), pl.ds(k * rows, rows)] = jnp.where(ids == expert, gates, 0.0)


def expert_kernel(
    cand_ref, stuff_ref, last_ref, up_ref, tower_ref, out_ref, total, turned
):
    step = pl.program_id(0)
    tile = up_ref.shape[1]
    peers, share, early = cand_ref.shape
    rows = peers * share

    @pl.when(step == 0)
    def _():
        total[...] = jnp.zeros_like(total)
        count = (last_ref.shape[1] - share // 2) // share
        scale = last_ref[:, pl.ds(count * share, share // 2), :].astype(F32)
        scale = scale.reshape(rows // 2, 128)
        scale = scale + pltpu.roll(scale, 127, 1)
        scale = scale.reshape(peers, share // 2, 128) * 0.5
        scale = jnp.concatenate([scale[:, :, 0:1], scale[:, :, 64:65]], axis=1)
        scale = jnp.broadcast_to(scale, (peers, share, 128))
        for i in range(early // 128):
            cols = pl.ds(i * 128, 128)
            block = cand_ref[:, :, cols].astype(F32) * 0.5
            block = block + stuff_ref[:, :, cols].astype(F32) * scale
            turned[cols, :] = jnp.transpose(block.astype(BF16).reshape(rows, 128))
        for i in range(count):
            block = last_ref[:, pl.ds(i * share, share), :].reshape(rows, 128)
            turned[pl.ds(early + i * 128, 128), :] = jnp.transpose(block * jnp.asarray(0.5, BF16))

    half = lax.dot_general(up_ref[...], turned[...], TN, preferred_element_type=F32)
    hidden = (half + half * jnp.tanh(half)).astype(BF16)
    tower = tower_ref[:, pl.ds(pl.multiple_of(step * tile, tile), tile)]
    total[...] += jnp.dot(tower, hidden, preferred_element_type=F32)

    @pl.when(step == pl.num_programs(0) - 1)
    def _():
        found = total[0:8, :] + total[8:16, :]
        each = 128 // share
        for peer in range(peers):
            out_ref[peer] = found[:, (peer // each) * 128 : (peer // each + 1) * 128]


def combine_kernel(slot_ref, weight_ref, back_ref, out_ref):
    rows = slot_ref.shape[1] // 2
    hot = slot_ref[...]
    back = back_ref[...]
    high = back.astype(BF16)
    rest = back - high.astype(F32)
    middle = rest.astype(BF16)
    low = (rest - middle.astype(F32)).astype(BF16)
    found = jnp.dot(high, hot, preferred_element_type=F32)
    found += jnp.dot(middle, hot, preferred_element_type=F32)
    found += jnp.dot(low, hot, preferred_element_type=F32)
    found = found * weight_ref[...]
    found = found[:, :rows] + found[:, rows:]
    total = found[0:8]
    for expert in range(1, found.shape[0] // 8):
        total = total + found[expert * 8 : (expert + 1) * 8]
    out_ref[...] = total[: out_ref.shape[0]]


def params():
    return pltpu.CompilerParams(vmem_limit_bytes=LIMIT)


def cost(flops, bytes_accessed, transcendentals=0):
    return pl.CostEstimate(flops=flops, bytes_accessed=bytes_accessed, transcendentals=transcendentals)


def whole(*shape):
    return pl.BlockSpec(shape, lambda i, *_: (0,) * len(shape))


def local(
    cand_emb,
    cand_request,
    hist_blocks,
    cache_kv,
    block_map,
    w_query_update,
    rel_bias,
    norm_gain,
    w_gate,
    expert_ids,
    w_up,
    w_down,
    w_tower,
):
    rows, feature = cand_emb.shape
    owners = lax.axis_size("req")
    me = lax.axis_index("req").astype(jnp.int32)
    head_count = rel_bias.shape[0]
    tasks = w_tower.shape[1]
    experts = w_gate.shape[1] // tasks
    capacity = 2 * rows * expert_ids.shape[1] // experts
    slots = experts * capacity
    heads = head_count // 2
    early = heads * 128
    keys = cache_kv.shape[0] // owners * cache_kv.shape[1]
    parts = 2 * heads
    me_scalar = me[None]
    smem = pl.BlockSpec(memory_space=pltpu.SMEM)

    cache = cache_kv.reshape(owners, keys, 2 * feature)

    def pack(chunk):
        def block(shift, half):
            return pl.BlockSpec(
                (1, keys, early),
                lambda i, me, ids: (lax.rem(me[0] + shift, owners), 0, 2 * half + chunk),
            )

        tail = 16 if chunk == 0 else 0
        shapes = [jax.ShapeDtypeStruct((parts * keys + tail, 128), BF16)] * len(SHIFTS)
        if chunk == 0:
            shapes.append(jax.ShapeDtypeStruct((16, 128), BF16))
        blocks = [block(shift, half) for shift in SHIFTS for half in range(2)]
        return pl.pallas_call(
            pack_kernel,
            grid_spec=pltpu.PrefetchScalarGridSpec(
                num_scalar_prefetch=2,
                grid=(1,),
                in_specs=blocks,
                out_specs=[whole(*shape.shape) for shape in shapes],
            ),
            out_shape=shapes,
            compiler_params=params(),
            cost_estimate=cost(0, 10**6),
            name="pack",
        )(me_scalar, block_map, *[cache] * len(blocks))

    def send(item, shift):
        pairs = [(i, (i + shift) % owners) for i in range(owners)]
        return lax.ppermute(item, "req", pairs)

    *packed, own_tile = pack(0)
    first_moved = [send(item, shift) for item, shift in zip(packed, SHIFTS)]
    packed_last = pack(1)
    last_moved = []
    for item, ahead, shift in zip(packed_last, first_moved, SHIFTS):
        item, _ = lax.optimization_barrier((item, ahead))
        last_moved.append(send(item, shift))

    ids_rows, _ = lax.optimization_barrier((expert_ids.T, own_tile))
    each = 128 // capacity
    lane = lax.rem(lax.axis_index("exp").astype(jnp.int32), each) * capacity
    place, slot_hot, cand_out = pl.pallas_call(
        functools.partial(route_kernel, capacity),
        grid=(1,),
        in_specs=[
            smem,
            whole(2, rows),
            pl.BlockSpec((rows, early), lambda i: (0, 0)),
        ],
        out_specs=[whole(slots, rows), whole(128, 2 * rows), whole(slots, early)],
        out_shape=[
            jax.ShapeDtypeStruct((slots, rows), BF16),
            jax.ShapeDtypeStruct((128, 2 * rows), BF16),
            jax.ShapeDtypeStruct((slots, early), BF16),
        ],
        compiler_params=params(),
        cost_estimate=cost(5 * 10**8, 3 * 10**6),
        name="route",
    )(lane[None], ids_rows, cand_emb)

    def exchange(item):
        return lax.all_to_all(item, "exp", split_axis=0, concat_axis=0, tiled=True)

    cand_in = exchange(cand_out.reshape(experts, capacity, early))

    cand_rows, _, _ = lax.optimization_barrier((cand_emb, place, packed_last[0]))
    steps = 4
    wide = 2 * feature // steps
    queries, update = pl.pallas_call(
        functools.partial(project_kernel, feature),
        grid=(steps,),
        in_specs=[whole(rows, feature), pl.BlockSpec((feature, wide), lambda i: (0, i))],
        out_specs=[
            pl.BlockSpec((rows, wide), lambda i: (0, jnp.minimum(i, 1))),
            pl.BlockSpec((rows, wide), lambda i: (0, jnp.maximum(i - 2, 0))),
        ],
        out_shape=[
            jax.ShapeDtypeStruct((rows, feature), BF16),
            jax.ShapeDtypeStruct((rows, feature), F32),
        ],
        compiler_params=params(),
        cost_estimate=cost(11 * 10**8, 6 * 10**6, 2**18),
        name="project",
    )(cand_rows, w_query_update)

    hidden_count = w_up.shape[2]
    tile = 512
    towers = pl.pallas_call(
        tower_kernel,
        grid=(hidden_count // tile,),
        in_specs=[
            pl.BlockSpec((None, tile, feature), lambda i: (0, i, 0)),
            whole(16, feature),
        ],
        out_specs=pl.BlockSpec((16, tile), lambda i: (0, i)),
        out_shape=jax.ShapeDtypeStruct((16, hidden_count), BF16),
        compiler_params=params(),
        cost_estimate=cost(10**8, 9 * 10**6),
        name="tower",
    )(w_down, jnp.pad(w_tower.T, ((0, 16 - tasks), (0, 0))))

    def attend_specs(chunk, moved):
        base = chunk * heads
        specs = [
            smem,
            smem,
            whole(rows, 1),
            pl.BlockSpec((rows, 128), lambda i, me: (0, base + i)),
            pl.BlockSpec((1, keys, 128), lambda i, me: (me[0], 0, base + i)),
            pl.BlockSpec((1, keys, 128), lambda i, me: (me[0], 0, head_count + base + i)),
        ]
        args = [hist_blocks, rel_bias, cand_request[:, None], queries, cache, cache]
        for item in moved:
            specs.append(pl.BlockSpec((keys, 128), lambda i, me: (i, 0)))
            specs.append(pl.BlockSpec((keys, 128), lambda i, me: (heads + i, 0)))
            args += [item, item]
        specs.append(whole(16, 128))
        args.append(own_tile)
        at = parts * keys // 16
        for item in first_moved:
            specs.append(pl.BlockSpec((16, 128), lambda i, me: (at, 0)))
            args.append(item)
        return specs, args

    gain = norm_gain[None, :]
    specs, args = attend_specs(0, first_moved)
    stuff_out, stuff, square = pl.pallas_call(
        attend_first_kernel,
        grid_spec=pltpu.PrefetchScalarGridSpec(
            num_scalar_prefetch=1,
            grid=(heads,),
            in_specs=[
                *specs,
                pl.BlockSpec((rows, 128), lambda i, me: (0, i)),
                pl.BlockSpec((1, 128), lambda i, me: (0, i)),
                whole(slots, rows),
            ],
            out_specs=[
                pl.BlockSpec((slots, 128), lambda i, me: (0, i)),
                pl.BlockSpec((rows, 128), lambda i, me: (0, i)),
                whole(rows, 128),
            ],
            scratch_shapes=[pltpu.VMEM((owners, rows, keys), BF16)],
        ),
        out_shape=[
            jax.ShapeDtypeStruct((slots, early), BF16),
            jax.ShapeDtypeStruct((rows, early), BF16),
            jax.ShapeDtypeStruct((rows, 128), F32),
        ],
        compiler_params=params(),
        cost_estimate=cost(30 * 10**9, 10**6),
        name="attend_first",
    )(me_scalar, *args, update, gain, place)

    stuff_in = exchange(stuff_out.reshape(experts, capacity, early))

    late = feature - early
    specs, args = attend_specs(1, last_moved)
    last_rows = (heads * capacity) + capacity // 2
    last_out, mixed_rows = pl.pallas_call(
        attend_last_kernel,
        grid_spec=pltpu.PrefetchScalarGridSpec(
            num_scalar_prefetch=1,
            grid=(heads,),
            in_specs=[
                *specs,
                pl.BlockSpec((rows, late), lambda i, me: (0, 1)),
                pl.BlockSpec((1, late), lambda i, me: (0, 1)),
                whole(slots, rows),
                whole(rows, feature),
                whole(rows, early),
                whole(rows, 128),
            ],
            out_specs=[whole(experts, last_rows, 128), whole(rows, feature)],
            scratch_shapes=[
                pltpu.VMEM((owners, rows, keys), BF16),
                pltpu.VMEM((heads, rows, 128), F32),
            ],
        ),
        out_shape=[
            jax.ShapeDtypeStruct((experts, last_rows, 128), BF16),
            jax.ShapeDtypeStruct((rows, feature), BF16),
        ],
        compiler_params=params(),
        cost_estimate=cost(100 * 10**9, 10**6),
        name="attend_last",
    )(me_scalar, *args, update, gain, place, cand_emb, stuff, square)

    last_in = exchange(last_out)

    gates = pl.pallas_call(
        functools.partial(gate_kernel, tasks),
        out_shape=jax.ShapeDtypeStruct((experts * 8, 2 * rows), F32),
        compiler_params=params(),
        cost_estimate=cost(10**8, 2 * 10**6, 4096),
        name="gate",
    )(ids_rows, w_gate.T, mixed_rows)

    produced = pl.pallas_call(
        expert_kernel,
        grid=(hidden_count // tile,),
        in_specs=[
            whole(experts, capacity, early),
            whole(experts, capacity, early),
            whole(experts, last_rows, 128),
            pl.BlockSpec((None, feature, tile), lambda i: (0, 0, i)),
            whole(16, hidden_count),
        ],
        out_specs=whole(experts, 8, 128),
        out_shape=jax.ShapeDtypeStruct((experts, 8, 128), F32),
        scratch_shapes=[pltpu.VMEM((16, slots), F32), pltpu.VMEM((feature, slots), BF16)],
        compiler_params=params(),
        cost_estimate=cost(11 * 10**9, 13 * 10**6, 2**22),
        name="expert",
    )(cand_in, stuff_in, last_in, w_up, towers)

    came_back = exchange(produced)

    scores = pl.pallas_call(
        combine_kernel,
        out_shape=jax.ShapeDtypeStruct((tasks, rows), F32),
        compiler_params=params(),
        cost_estimate=cost(10**8, 10**6),
        name="combine",
    )(slot_hot, gates, came_back.reshape(experts * 8, 128))
    return scores.T


def solution(mesh):
    placed = (
        P(("req", "exp"), None),
        P(("req", "exp")),
        P(("req", "exp")),
        P(("req", "exp"), None, None),
        P(("req", "exp")),
        P(),
        P(),
        P(),
        P(),
        P(("req", "exp"), None),
        P("exp", None, None),
        P("exp", None, None),
        P(),
    )
    return jax.shard_map(
        local, mesh=mesh, in_specs=placed, out_specs=P(("req", "exp"), None), check_vma=False
    )
```

```python
import functools
import math

import jax
import jax.numpy as jnp
from jax import lax
from jax.experimental import pallas as pl
from jax.experimental.pallas import tpu as pltpu
from jax.sharding import PartitionSpec as P

EPSILON = 1e-05
F32 = jnp.float32
BF16 = jnp.bfloat16
NT = (((1,), (1,)), ((), ()))
TN = (((0,), (0,)), ((), ()))
SHIFTS = (1, 3, 2)
LIMIT = 63 * 2**20
AHEAD = 3
FIRST_COST = 30 * 10**9
EARLY_COST = 5 * 10**9
LAST_COST = 100 * 10**9


def pack_kernel(me_ref, ids_ref, *refs):
    count = len(SHIFTS)
    ins, outs = refs[: 2 * count], refs[2 * count :]
    keys = ins[0].shape[1]
    heads = ins[0].shape[2] // 128
    for n, shift in enumerate(SHIFTS):
        for head in range(heads):
            cols = pl.ds(head * 128, 128)
            outs[n][pl.ds(head * keys, keys), :] = ins[2 * n][0, :, cols]
            outs[n][pl.ds((heads + head) * keys, keys), :] = ins[2 * n + 1][0, :, cols]
    if len(outs) > count:
        row = lax.broadcasted_iota(jnp.int32, (16, 128), 0)
        me = me_ref[0]

        def tile_of(owner):
            first = ids_ref[2 * owner].astype(F32)
            second = ids_ref[2 * owner + 1].astype(F32)
            return jnp.where(row == 0, first, second).astype(BF16)

        for n, shift in enumerate(SHIFTS):
            outs[n][pl.ds(2 * heads * keys, 16), :] = tile_of(lax.rem(me + shift, count + 1))
        outs[count][...] = tile_of(me)


def route_kernel(capacity, lane_ref, ids_ref, req_ref, cand_ref, place_ref, slot_ref, first_ref, out_ref):
    rows = ids_ref.shape[1]
    experts = place_ref.shape[0] // capacity
    ids = jnp.concatenate([ids_ref[0:1, :], ids_ref[1:2, :]], axis=1)
    hot = lax.broadcasted_iota(jnp.int32, (experts, 2 * rows), 0) == ids
    hot = jnp.where(hot, 1.0, 0.0)
    here = lax.broadcasted_iota(jnp.int32, (2 * rows, 2 * rows), 0)
    there = lax.broadcasted_iota(jnp.int32, (2 * rows, 2 * rows), 1)
    earlier = jnp.where(here < there, 1.0, 0.0).astype(BF16)
    counts = jnp.dot(hot.astype(BF16), earlier, preferred_element_type=F32)
    position = jnp.sum(counts * hot, axis=0, keepdims=True).astype(jnp.int32)
    slot = ids * capacity + position
    spot = lax.broadcasted_iota(jnp.int32, place_ref.shape, 0)
    place = (spot == slot[:, :rows]) | (spot == slot[:, rows:])
    place = jnp.where(place, 1.0, 0.0).astype(BF16)
    place_ref[...] = place
    lane = position + lane_ref[0]
    lanes = lax.broadcasted_iota(jnp.int32, slot_ref.shape, 0) == lane
    slot_ref[...] = jnp.where(lanes, 1.0, 0.0).astype(BF16)
    out_ref[...] = jnp.dot(place, cand_ref[...], preferred_element_type=F32).astype(BF16)
    first = jnp.where(req_ref[...] == 0, 1.0, 0.0)
    first_ref[...] = jnp.transpose(jnp.broadcast_to(first, (128, rows))).astype(BF16)


def project_kernel(cand_ref, weight_ref, gain_ref, query_ref, update_ref):
    step = pl.program_id(0)
    half = pl.num_programs(0) // 2
    projected = jnp.dot(cand_ref[...], weight_ref[...], preferred_element_type=F32)

    @pl.when(step < half)
    def _():
        query_ref[...] = projected.astype(BF16)

    @pl.when(step >= half)
    def _():
        update_ref[...] = gain_ref[...] * projected / (1.0 + jnp.exp(-projected))


def tower_kernel(down_at, tower_ref, out_ref, down, sems):
    count, tile, _ = down.shape
    loads = []
    for i in range(count):
        here = pl.ds(i * tile, tile)
        loads.append(pltpu.make_async_copy(down_at.at[0, here, :], down.at[i], sems.at[i]))
    for i in range(2):
        loads[i].start()
    for i in range(count):
        if i + 2 < count:
            loads[i + 2].start()
        loads[i].wait()
        product = lax.dot_general(tower_ref[...], down[i], NT, preferred_element_type=F32)
        high = product.astype(BF16)
        low = (product - high.astype(F32)).astype(BF16)
        out_ref[:, pl.ds(i * tile, tile)] = jnp.concatenate([high[0:8], low[0:8]], axis=0)


def attend_head(head, first, mask, query, key, value, blocks, bias_ref):
    scores = lax.dot_general(query, key, NT, preferred_element_type=F32)
    weights = []
    for owner, (block_a, block_b) in enumerate(blocks):
        here = scores[:, owner * 256 : (owner + 1) * 256]
        here = jnp.where(first, here[:, :128], here[:, 128:])
        bias_a = jnp.zeros_like(block_a)
        bias_b = jnp.zeros_like(block_b)
        for block in range(bias_ref.shape[0]):
            entry = bias_ref[block, head] * 0.5
            bias_a = jnp.where(block_a == block, entry, bias_a)
            bias_b = jnp.where(block_b == block, entry, bias_b)
        half = here * (0.5 / math.sqrt(128.0)) + jnp.where(first, bias_a, bias_b)
        weight = (half + half * jnp.tanh(half)).astype(BF16)
        weights += [weight, weight]
    weights = jnp.concatenate(weights, axis=1) * mask
    return jnp.dot(weights, value, preferred_element_type=F32)


def attend_kernel(chunk, me_ref, hist_ref, bias_ref, *refs):
    last = chunk == 1
    query_at, cache_at, *refs = refs
    moved_at, refs = refs[:3], refs[3:]
    ids_at, refs = refs[:3], refs[3:]
    own_at, first_at, update_at, place_at, *refs = refs
    if last:
        cand_at, stuff_at, square_at, *refs = refs
        out_at, mixed_at, *refs = refs
    else:
        out_at, stuff_at, square_at, *refs = refs
    sems, kv, tiles, query, first_in, update, place, square, stuff, out, *refs = refs
    if last:
        cand, mixed, attended = refs
    owners, keys, width = cache_at.shape
    parts = kv.shape[0]
    heads = parts // 2
    early = heads * 128
    base = chunk * heads
    rows = query.shape[0]
    me = me_ref[0]
    used = []

    def copy(source, target):
        item = pltpu.make_async_copy(source, target, sems.at[len(used)])
        item.start()
        used.append(item)
        return item

    wanted = [copy(query_at.at[:, pl.ds(base * 128, early)], query)]
    wanted.append(copy(first_at, first_in))
    wanted.append(copy(own_at, tiles.at[0]))
    for n in range(3):
        wanted.append(copy(ids_at[n].at[pl.ds(parts * keys, 16), :], tiles.at[n + 1]))
    loads = []
    for head in range(heads):
        load = []
        for half in range(2):
            part = half * heads + head
            col = half * (width // 2) + (base + head) * 128
            load.append(copy(cache_at.at[me, :, pl.ds(col, 128)], kv.at[part, 0]))
            for n in range(3):
                load.append(copy(moved_at[n].at[pl.ds(part * keys, keys), :], kv.at[part, n + 1]))
        loads.append(load)
        if head == 0:
            later = [copy(update_at.at[:, pl.ds(base * 128, early)], update), copy(place_at, place)]
    if last:
        later += [copy(cand_at, cand), copy(stuff_at, stuff), copy(square_at, square)]
    for item in wanted:
        item.wait()
    first = first_in[...].astype(F32) > 0.5
    length_a = hist_ref[0].astype(F32)
    length_b = hist_ref[1].astype(F32)
    blocks = []
    masks = []
    for owner in range(owners):
        tile = tiles[owner].astype(F32)
        block_a, block_b = tile[0:1, :], tile[1:2, :]
        blocks.append((block_a, block_b))
        mask_a = jnp.where(first, jnp.where(block_a < length_a, 1.0, 0.0), 0.0)
        mask_b = jnp.where(first, 0.0, jnp.where(block_b < length_b, 1.0, 0.0))
        masks += [mask_a.astype(BF16), mask_b.astype(BF16)]
    mask = jnp.concatenate(masks, axis=1)
    total = None
    stores = []
    for load in loads:
        for item in load:
            item.wait()
    for item in later:
        item.wait()
    for head in range(heads):
        cols = pl.ds(head * 128, 128)
        key = kv[head].reshape(owners * keys, 128)
        value = kv[heads + head].reshape(owners * keys, 128)
        found = attend_head(base + head, first, mask, query[:, cols], key, value, blocks, bias_ref)
        total = found * found if total is None else total + found * found
        if last:
            attended[:, cols] = found * update[:, cols]
            continue
        stuff[:, cols] = (found * update[:, cols]).astype(BF16)
        if head % 2 == 1:
            here = pl.ds((head - 1) * 128, 256)
            out[:, here] = jnp.dot(place[...], stuff[:, here], preferred_element_type=F32).astype(BF16)
            stores.append(copy(out.at[:, here], out_at.at[:, here]))
    if not last:
        square[...] = total
        stores.append(copy(stuff, stuff_at))
        stores.append(copy(square, square_at))
        for item in stores:
            item.wait()
        return
    feature = cand.shape[1]
    mean = jnp.sum(total + square[...], axis=1, keepdims=True) * (1.0 / feature)
    inv_rms = lax.rsqrt(mean + EPSILON)
    peers = out.shape[0]
    share = place.shape[0] // peers
    for i in range(heads // 2):
        cols = pl.ds(early + i * 256, 256)
        block = cand[:, cols].astype(F32) + attended[:, pl.ds(i * 256, 256)] * inv_rms
        block = block.astype(BF16)
        mixed[:, cols] = block
        sent = jnp.dot(place[...], block, preferred_element_type=F32).astype(BF16)
        for j in range(2):
            here = pl.ds((2 * i + j) * share, share)
            out[:, here, :] = sent[:, j * 128 : (j + 1) * 128].reshape(peers, share, 128)
    scale = jnp.transpose(jnp.broadcast_to(inv_rms, (rows, 128)))[0:16, :]
    high = scale.astype(BF16).astype(F32)
    row = lax.broadcasted_iota(jnp.int32, scale.shape, 0)
    scale = jnp.where(row == 0, high, jnp.where(row == 1, scale - high, 0.0)).astype(BF16)
    scale = lax.dot_general(scale, place[...], NT, preferred_element_type=F32)
    each = 128 // share
    for peer in range(peers):
        tile = scale[:, (peer // each) * 128 : (peer // each + 1) * 128]
        if peer % each:
            tile = pltpu.roll(tile, 128 - (peer % each) * share, 1)
        out[peer, pl.ds(heads * share, 16), :] = tile.astype(BF16)
    stores.append(copy(out, out_at))
    mixed[:, :early] = (cand[:, :early].astype(F32) + stuff[...].astype(F32) * inv_rms).astype(BF16)
    stores.append(copy(mixed, mixed_at))
    for item in stores:
        item.wait()


def gate_kernel(tasks, ids_ref, weight_ref, mixed_ref, out_ref):
    rows = mixed_ref.shape[0]
    experts = weight_ref.shape[0] // tasks
    logits = lax.dot_general(weight_ref[...], mixed_ref[...], NT, preferred_element_type=F32)
    squashed = []
    for k in range(2):
        hot = lax.broadcasted_iota(jnp.int32, (experts, rows), 0) == ids_ref[k : k + 1, :]
        picked = []
        for task in range(8):
            if task < tasks:
                here = logits[task * experts : (task + 1) * experts, :]
                picked.append(jnp.sum(jnp.where(hot, here, 0.0), axis=0, keepdims=True))
            else:
                picked.append(jnp.zeros((1, rows), F32))
        squashed.append(jax.nn.sigmoid(jnp.concatenate(picked, axis=0)))
    whole = squashed[0] + squashed[1]
    for k in range(2):
        gates = squashed[k] / whole
        ids = ids_ref[k : k + 1, :]
        for expert in range(experts):
            out_ref[pl.ds(expert * 8, 8), pl.ds(k * rows, rows)] = jnp.where(ids == expert, gates, 0.0)


def early_kernel(rows_at, up_at, out_at, rows, up, turned, out, sems):
    peers, share, early = rows.shape
    count, _, tile = up.shape
    fetch = pltpu.make_async_copy(rows_at, rows, sems.at[0])
    fetch.start()
    ups = []
    for i in range(count):
        here = pl.ds(i * tile, tile)
        ups.append(pltpu.make_async_copy(up_at.at[0, pl.ds(0, early), here], up.at[i], sems.at[i + 1]))
    ups[0].start()
    fetch.wait()
    for i in range(early // 128):
        cols = pl.ds(i * 128, 128)
        block = rows[:, :, cols].reshape(peers * share, 128)
        turned[cols, :] = jnp.transpose(block * jnp.asarray(0.5, BF16))
    stores = []
    for i in range(count):
        ups[i].wait()
        if i + 1 < count:
            ups[i + 1].start()
        found = lax.dot_general(up[i], turned[...], TN, preferred_element_type=F32)
        out[i] = found.astype(BF16)
        store = pltpu.make_async_copy(out.at[i], out_at.at[pl.ds(i * tile, tile), :], sems.at[count + 1 + i])
        store.start()
        stores.append(store)
    for store in stores:
        store.wait()


def expert_kernel(
    last_at, cand_at, stuff_at, up_at, tower_at, out_ref, last, cand, stuff, up, tower, turned, scale, sems
):
    count, late, tile = up.shape
    peers = last.shape[0]
    share = (last.shape[1] - 16) // (late // 128)
    rows = peers * share
    each = 128 // share
    fetch = pltpu.make_async_copy(last_at, last, sems.at[0])
    fetch.start()
    loads = []
    for i in range(count):
        here = pl.ds(i * tile, tile)
        loads.append(
            (
                pltpu.make_async_copy(up_at.at[0, pl.ds(late, late), here], up.at[i], sems.at[3 * i + 2]),
                pltpu.make_async_copy(cand_at.at[here, :], cand.at[i], sems.at[3 * i + 3]),
                pltpu.make_async_copy(stuff_at.at[here, :], stuff.at[i], sems.at[3 * i + 4]),
            )
        )
    fetch_tower = pltpu.make_async_copy(tower_at, tower, sems.at[1])
    fetch_tower.start()
    for ahead in range(AHEAD):
        for item in loads[ahead]:
            item.start()
    fetch.wait()
    for i in range(late // 128):
        block = last[:, pl.ds(i * share, share), :].reshape(rows, 128)
        turned[pl.ds(i * 128, 128), :] = jnp.transpose(block * jnp.asarray(0.5, BF16))
    lane = lax.broadcasted_iota(jnp.int32, (16, 128), 1)
    for group in range(peers // each):
        whole_tile = None
        for i in range(each):
            part = last[group * each + i, pl.ds(late // 128 * share, 16), :].astype(F32)
            part = pltpu.roll(part, i * share, 1) if i else part
            part = jnp.where((lane >= i * share) & (lane < (i + 1) * share), part, 0.0)
            whole_tile = part if whole_tile is None else whole_tile + part
        scale[:, pl.ds(group * 128, 128)] = whole_tile[0:1, :] + whole_tile[1:2, :]
    fetch_tower.wait()
    total = None
    for i in range(count):
        if i + AHEAD < count:
            for item in loads[i + AHEAD]:
                item.start()
        for item in loads[i]:
            item.wait()
        half = lax.dot_general(up[i], turned[...], TN, preferred_element_type=F32)
        half = half + cand[i].astype(F32) + stuff[i].astype(F32) * scale[...]
        hidden = (half + half * jnp.tanh(half)).astype(BF16)
        part = jnp.dot(tower[:, pl.ds(i * tile, tile)], hidden, preferred_element_type=F32)
        total = part if total is None else total + part
    found = total[0:8, :] + total[8:16, :]
    for peer in range(peers):
        out_ref[peer] = found[:, (peer // each) * 128 : (peer // each + 1) * 128]


def combine_kernel(slot_ref, weight_ref, back_ref, out_ref):
    rows = slot_ref.shape[1] // 2
    hot = slot_ref[...]
    back = back_ref[...]
    high = back.astype(BF16)
    rest = back - high.astype(F32)
    middle = rest.astype(BF16)
    low = (rest - middle.astype(F32)).astype(BF16)
    found = jnp.dot(high, hot, preferred_element_type=F32)
    found += jnp.dot(middle, hot, preferred_element_type=F32)
    found += jnp.dot(low, hot, preferred_element_type=F32)
    found = found * weight_ref[...]
    found = found[:, :rows] + found[:, rows:]
    total = found[0:8]
    for expert in range(1, found.shape[0] // 8):
        total = total + found[expert * 8 : (expert + 1) * 8]
    out_ref[...] = total[: out_ref.shape[0]]


def params():
    return pltpu.CompilerParams(vmem_limit_bytes=LIMIT)


def cost(flops, bytes_accessed, transcendentals=0):
    return pl.CostEstimate(flops=flops, bytes_accessed=bytes_accessed, transcendentals=transcendentals)


def whole(*shape):
    return pl.BlockSpec(shape, lambda i, *_: (0,) * len(shape))


def local(
    cand_emb,
    cand_request,
    hist_blocks,
    cache_kv,
    block_map,
    w_query_update,
    rel_bias,
    norm_gain,
    w_gate,
    expert_ids,
    w_up,
    w_down,
    w_tower,
):
    rows, feature = cand_emb.shape
    owners = lax.axis_size("req")
    me = lax.axis_index("req").astype(jnp.int32)
    head_count = rel_bias.shape[0]
    tasks = w_tower.shape[1]
    experts = w_gate.shape[1] // tasks
    capacity = 2 * rows * expert_ids.shape[1] // experts
    slots = experts * capacity
    heads = head_count // 2
    early = heads * 128
    keys = cache_kv.shape[0] // owners * cache_kv.shape[1]
    parts = 2 * heads
    me_scalar = me[None]
    smem = pl.BlockSpec(memory_space=pltpu.SMEM)

    cache = cache_kv.reshape(owners, keys, 2 * feature)

    def pack(chunk):
        def block(shift, half):
            return pl.BlockSpec(
                (1, keys, early),
                lambda i, me, ids: (lax.rem(me[0] + shift, owners), 0, 2 * half + chunk),
            )

        tail = 16 if chunk == 0 else 0
        shapes = [jax.ShapeDtypeStruct((parts * keys + tail, 128), BF16)] * len(SHIFTS)
        if chunk == 0:
            shapes.append(jax.ShapeDtypeStruct((16, 128), BF16))
        blocks = [block(shift, half) for shift in SHIFTS for half in range(2)]
        return pl.pallas_call(
            pack_kernel,
            grid_spec=pltpu.PrefetchScalarGridSpec(
                num_scalar_prefetch=2,
                grid=(1,),
                in_specs=blocks,
                out_specs=[whole(*shape.shape) for shape in shapes],
            ),
            out_shape=shapes,
            compiler_params=params(),
            cost_estimate=cost(0, 10**6),
            name="pack",
        )(me_scalar, block_map, *[cache] * len(blocks))

    def send(item, shift):
        pairs = [(i, (i + shift) % owners) for i in range(owners)]
        return lax.ppermute(item, "req", pairs)

    *packed, own_tile = pack(0)
    first_moved = [send(item, shift) for item, shift in zip(packed, SHIFTS)]
    packed_last = pack(1)
    last_moved = []
    for item, ahead, shift in zip(packed_last, first_moved, SHIFTS):
        item, _ = lax.optimization_barrier((item, ahead))
        last_moved.append(send(item, shift))

    ids_rows, _ = lax.optimization_barrier((expert_ids.T, own_tile))
    each = 128 // capacity
    lane = lax.rem(lax.axis_index("exp").astype(jnp.int32), each) * capacity
    place, slot_hot, first, cand_out = pl.pallas_call(
        functools.partial(route_kernel, capacity),
        grid=(1,),
        in_specs=[
            smem,
            whole(2, rows),
            whole(1, rows),
            pl.BlockSpec((rows, early), lambda i: (0, 0)),
        ],
        out_specs=[whole(slots, rows), whole(128, 2 * rows), whole(rows, 128), whole(slots, early)],
        out_shape=[
            jax.ShapeDtypeStruct((slots, rows), BF16),
            jax.ShapeDtypeStruct((128, 2 * rows), BF16),
            jax.ShapeDtypeStruct((rows, 128), BF16),
            jax.ShapeDtypeStruct((slots, early), BF16),
        ],
        compiler_params=params(),
        cost_estimate=cost(5 * 10**8, 3 * 10**6),
        name="route",
    )(lane[None], ids_rows, cand_request[None, :], cand_emb)

    def exchange(item):
        return lax.all_to_all(item, "exp", split_axis=0, concat_axis=0, tiled=True)

    cand_in = exchange(cand_out.reshape(experts, capacity, early))

    cand_rows, _, _ = lax.optimization_barrier((cand_emb, place, packed_last[0]))
    steps = 4
    wide = 2 * feature // steps
    queries, update = pl.pallas_call(
        project_kernel,
        grid=(steps,),
        in_specs=[
            whole(rows, feature),
            pl.BlockSpec((feature, wide), lambda i: (0, i)),
            pl.BlockSpec((1, wide), lambda i: (0, jnp.maximum(i - 2, 0))),
        ],
        out_specs=[
            pl.BlockSpec((rows, wide), lambda i: (0, jnp.minimum(i, 1))),
            pl.BlockSpec((rows, wide), lambda i: (0, jnp.maximum(i - 2, 0))),
        ],
        out_shape=[
            jax.ShapeDtypeStruct((rows, feature), BF16),
            jax.ShapeDtypeStruct((rows, feature), F32),
        ],
        compiler_params=params(),
        cost_estimate=cost(11 * 10**8, 6 * 10**6, 2**18),
        name="project",
    )(cand_rows, w_query_update, norm_gain[None, :])

    hidden_count = w_up.shape[2]
    tile = 512
    towers = pl.pallas_call(
        tower_kernel,
        in_specs=[pl.BlockSpec(memory_space=pl.ANY), pl.BlockSpec(memory_space=pltpu.VMEM)],
        out_shape=jax.ShapeDtypeStruct((16, hidden_count), BF16),
        scratch_shapes=[
            pltpu.VMEM((hidden_count // tile, tile, feature), BF16),
            pltpu.SemaphoreType.DMA((hidden_count // tile,)),
        ],
        compiler_params=params(),
        cost_estimate=cost(10**8, 9 * 10**6),
        name="tower",
    )(w_down, jnp.pad(w_tower.T, ((0, 16 - tasks), (0, 0))))

    anywhere = pl.BlockSpec(memory_space=pl.ANY)
    hbm = pl.BlockSpec(memory_space=pltpu.HBM)

    def attend(chunk, moved, extra, out_shape, extra_scratch, name, flops):
        arrays = [queries, cache, *moved, *first_moved, own_tile, first, update, place, *extra]
        out_rows = out_shape[0].shape
        return pl.pallas_call(
            functools.partial(attend_kernel, chunk),
            in_specs=[smem] * 3 + [anywhere] * 2 + [hbm] * 6 + [anywhere] * (len(arrays) - 8),
            out_specs=[anywhere] * len(out_shape),
            out_shape=out_shape,
            scratch_shapes=[
                pltpu.SemaphoreType.DMA((16 + 8 * heads,)),
                pltpu.VMEM((parts, owners, keys, 128), BF16),
                pltpu.VMEM((owners, 16, 128), BF16),
                pltpu.VMEM((rows, early), BF16),
                pltpu.VMEM((rows, 128), BF16),
                pltpu.VMEM((rows, early), F32),
                pltpu.VMEM((slots, rows), BF16),
                pltpu.VMEM((rows, 128), F32),
                pltpu.VMEM((rows, early), BF16),
                pltpu.VMEM(out_rows, BF16),
                *extra_scratch,
            ],
            compiler_params=params(),
            cost_estimate=cost(flops, 10**6),
            name=name,
        )(me_scalar, hist_blocks, rel_bias.T, *arrays)

    stuff_out, stuff, square = attend(
        0,
        first_moved,
        [],
        [
            jax.ShapeDtypeStruct((slots, early), BF16),
            jax.ShapeDtypeStruct((rows, early), BF16),
            jax.ShapeDtypeStruct((rows, 128), F32),
        ],
        [],
        "attend_first",
        FIRST_COST,
    )
    stuff_in = exchange(stuff_out.reshape(experts, capacity, early))

    def early_product(item, name):
        count = 4
        wide = hidden_count // count
        return pl.pallas_call(
            early_kernel,
            in_specs=[hbm, anywhere],
            out_specs=anywhere,
            out_shape=jax.ShapeDtypeStruct((hidden_count, slots), BF16),
            scratch_shapes=[
                pltpu.VMEM((experts, capacity, early), BF16),
                pltpu.VMEM((count, early, wide), BF16),
                pltpu.VMEM((early, slots), BF16),
                pltpu.VMEM((count, wide, slots), BF16),
                pltpu.SemaphoreType.DMA((2 * count + 1,)),
            ],
            compiler_params=params(),
            cost_estimate=cost(EARLY_COST, 10**6),
            name=name,
        )(item, w_up)

    cand_product = early_product(cand_in, "early_cand")
    square, _ = lax.optimization_barrier((square, cand_product))
    last_rows = heads * capacity + 16
    last_out, mixed_rows = attend(
        1,
        last_moved,
        [cand_emb, stuff, square],
        [
            jax.ShapeDtypeStruct((experts, last_rows, 128), BF16),
            jax.ShapeDtypeStruct((rows, feature), BF16),
        ],
        [
            pltpu.VMEM((rows, feature), BF16),
            pltpu.VMEM((rows, feature), BF16),
            pltpu.VMEM((rows, early), F32),
        ],
        "attend_last",
        LAST_COST,
    )
    last_in = exchange(last_out)
    stuff_product = early_product(stuff_in, "early_stuff")

    gates = pl.pallas_call(
        functools.partial(gate_kernel, tasks),
        out_shape=jax.ShapeDtypeStruct((experts * 8, 2 * rows), F32),
        compiler_params=params(),
        cost_estimate=cost(10**8, 2 * 10**6, 4096),
        name="gate",
    )(ids_rows, w_gate.T, mixed_rows)

    late = feature - early
    late = feature - early
    count = hidden_count // tile
    produced = pl.pallas_call(
        expert_kernel,
        in_specs=[hbm, anywhere, anywhere, anywhere, anywhere],
        out_shape=jax.ShapeDtypeStruct((experts, 8, 128), F32),
        scratch_shapes=[
            pltpu.VMEM((experts, last_rows, 128), BF16),
            pltpu.VMEM((count, tile, slots), BF16),
            pltpu.VMEM((count, tile, slots), BF16),
            pltpu.VMEM((count, late, tile), BF16),
            pltpu.VMEM((16, hidden_count), BF16),
            pltpu.VMEM((late, slots), BF16),
            pltpu.VMEM((1, slots), F32),
            pltpu.SemaphoreType.DMA((3 * count + 2,)),
        ],
        compiler_params=params(),
        cost_estimate=cost(6 * 10**9, 25 * 10**6, 2**22),
        name="expert",
    )(last_in, cand_product, stuff_product, w_up, towers)

    came_back = exchange(produced)

    scores = pl.pallas_call(
        combine_kernel,
        out_shape=jax.ShapeDtypeStruct((tasks, rows), F32),
        compiler_params=params(),
        cost_estimate=cost(10**8, 10**6),
        name="combine",
    )(slot_hot, gates, came_back.reshape(experts * 8, 128))
    return scores.T


def solution(mesh):
    placed = (
        P(("req", "exp"), None),
        P(("req", "exp")),
        P(("req", "exp")),
        P(("req", "exp"), None, None),
        P(("req", "exp")),
        P(),
        P(),
        P(),
        P(),
        P(("req", "exp"), None),
        P("exp", None, None),
        P("exp", None, None),
        P(),
    )
    return jax.shard_map(
        local, mesh=mesh, in_specs=placed, out_specs=P(("req", "exp"), None), check_vma=False
    )
```

```python
import functools
import math

import jax
import jax.numpy as jnp
from jax import lax
from jax.experimental import pallas as pl
from jax.experimental.pallas import tpu as pltpu
from jax.sharding import PartitionSpec as P

EPSILON = 1e-05
F32 = jnp.float32
BF16 = jnp.bfloat16
NT = (((1,), (1,)), ((), ()))
TN = (((0,), (0,)), ((), ()))
SHIFTS = (1, 3, 2)
HEADS_FIRST = 4
GATE_LIMIT = 8
COMBINE_LIMIT = 8
AHEAD = 3
FIRST_COST = 30 * 10**9
EARLY_COST = 5 * 10**9
LAST_COST = 100 * 10**9


def pack_kernel(chunk, me_ref, ids_ref, cache_at, *refs):
    count = len(SHIFTS)
    packed, sems = refs[-2:]
    outs = refs[:-2]
    owners, keys, width = cache_at.shape
    parts = packed.shape[1] // keys
    heads = parts // 2
    first = chunk * (width // 256 - heads)
    me = me_ref[0]
    loads = []
    for n, shift in enumerate(SHIFTS):
        to = lax.rem(me + shift, owners)
        for part in range(parts):
            col = (first + part % heads) * 128 + (part // heads) * (width // 2)
            here = packed.at[n, pl.ds(part * keys, keys), :]
            load = pltpu.make_async_copy(cache_at.at[to, :, pl.ds(col, 128)], here, sems.at[0, n, part])
            load.start()
            store = pltpu.make_async_copy(here, outs[n].at[pl.ds(part * keys, keys), :], sems.at[1, n, part])
            loads.append((load, store))
    stores = []
    if len(outs) > count:
        row = lax.broadcasted_iota(jnp.int32, (16, 128), 0)

        def tile_of(owner):
            one = ids_ref[2 * owner].astype(F32)
            two = ids_ref[2 * owner + 1].astype(F32)
            return jnp.where(row == 0, one, two).astype(BF16)

        for n, shift in enumerate(SHIFTS):
            here = pl.ds(parts * keys, 16)
            packed[n, here, :] = tile_of(lax.rem(me + shift, owners))
            store = pltpu.make_async_copy(packed.at[n, here, :], outs[n].at[here, :], sems.at[1, n, parts])
            store.start()
            stores.append(store)
        outs[count][...] = tile_of(me)
    for load, store in loads:
        load.wait()
        store.start()
        stores.append(store)
    for store in stores:
        store.wait()


def place_of(slot, slots):
    rows = slot.shape[1] // 2
    spot = lax.broadcasted_iota(jnp.int32, (slots, rows), 0)
    place = (spot == slot[:, :rows]) | (spot == slot[:, rows:])
    return jnp.where(place, 1.0, 0.0).astype(BF16)


def route_kernel(capacity, ids_ref, req_ref, cand_ref, spot_ref, first_ref, out_ref):
    rows = ids_ref.shape[1]
    experts = out_ref.shape[0] // capacity
    ids = jnp.concatenate([ids_ref[0:1, :], ids_ref[1:2, :]], axis=1)
    hot = lax.broadcasted_iota(jnp.int32, (experts, 2 * rows), 0) == ids
    hot = jnp.where(hot, 1.0, 0.0)
    here = lax.broadcasted_iota(jnp.int32, (2 * rows, 2 * rows), 0)
    there = lax.broadcasted_iota(jnp.int32, (2 * rows, 2 * rows), 1)
    earlier = jnp.where(here < there, 1.0, 0.0).astype(BF16)
    counts = jnp.dot(hot.astype(BF16), earlier, preferred_element_type=F32)
    position = jnp.sum(counts * hot, axis=0, keepdims=True).astype(jnp.int32)
    slot = ids * capacity + position
    spot_ref[...] = jnp.broadcast_to(slot, spot_ref.shape)
    place = place_of(slot, out_ref.shape[0])
    out_ref[...] = jnp.dot(place, cand_ref[...], preferred_element_type=F32).astype(BF16)
    first = jnp.where(req_ref[...] == 0, 1.0, 0.0)
    first_ref[...] = jnp.transpose(jnp.broadcast_to(first, (128, rows))).astype(BF16)


def project_kernel(cand_ref, weight_at, gain_ref, query_ref, update_ref, weight, sems):
    count, _, wide = weight.shape
    loads = []
    for i in range(count):
        here = pl.ds(i * wide, wide)
        loads.append(pltpu.make_async_copy(weight_at.at[:, here], weight.at[i], sems.at[i]))
        loads[i].start()
    for i in range(count):
        loads[i].wait()
        projected = jnp.dot(cand_ref[...], weight[i], preferred_element_type=F32)
        cols = pl.ds(i % (count // 2) * wide, wide)
        if i < count // 2:
            query_ref[:, cols] = projected.astype(BF16)
        else:
            update_ref[:, cols] = gain_ref[:, cols] * projected / (1.0 + jnp.exp(-projected))


def tower_kernel(down_at, tower_ref, out_ref, down, sems):
    count, tile, _ = down.shape
    loads = []
    for i in range(count):
        here = pl.ds(i * tile, tile)
        loads.append(pltpu.make_async_copy(down_at.at[0, here, :], down.at[i], sems.at[i]))
    for i in range(2):
        loads[i].start()
    for i in range(count):
        if i + 2 < count:
            loads[i + 2].start()
        loads[i].wait()
        product = lax.dot_general(tower_ref[...], down[i], NT, preferred_element_type=F32)
        high = product.astype(BF16)
        low = (product - high.astype(F32)).astype(BF16)
        out_ref[:, pl.ds(i * tile, tile)] = jnp.concatenate([high[0:8], low[0:8]], axis=0)


def attend_head(head, first, mask, query, key, value, blocks, bias_ref):
    scores = lax.dot_general(query, key, NT, preferred_element_type=F32)
    weights = []
    for owner, (block_a, block_b) in enumerate(blocks):
        here = scores[:, owner * 256 : (owner + 1) * 256]
        here = jnp.where(first, here[:, :128], here[:, 128:])
        bias_a = jnp.zeros_like(block_a)
        bias_b = jnp.zeros_like(block_b)
        for block in range(bias_ref.shape[0]):
            entry = bias_ref[block, head] * 0.5
            bias_a = jnp.where(block_a == block, entry, bias_a)
            bias_b = jnp.where(block_b == block, entry, bias_b)
        half = here * (0.5 / math.sqrt(128.0)) + jnp.where(first, bias_a, bias_b)
        weight = (half + half * jnp.tanh(half)).astype(BF16)
        weights += [weight, weight]
    weights = jnp.concatenate(weights, axis=1) * mask
    return jnp.dot(weights, value, preferred_element_type=F32)


def attend_kernel(chunk, me_ref, hist_ref, bias_ref, *refs):
    last = chunk == 1
    query_at, cache_at, *refs = refs
    moved_at, refs = refs[:3], refs[3:]
    ids_at, refs = refs[:3], refs[3:]
    own_at, first_at, update_at, spot_at, *refs = refs
    if last:
        cand_at, square_at, *refs = refs
        out_at, mixed_at, scale_at, *refs = refs
    else:
        out_at, stuff_at, square_at, *refs = refs
    sems, kv, own, tiles, query, first_in, update, spot, place, square, stuff, out, *refs = refs
    if last:
        cand, attended = refs
    owners, keys, width = cache_at.shape
    heads = own.shape[2] // 128
    early = heads * 128
    base = chunk * (width // 256 - heads)
    id_row = ids_at[0].shape[0] - 16
    rows = query.shape[0]
    me = me_ref[0]
    used = []

    def copy(source, target):
        item = pltpu.make_async_copy(source, target, sems.at[len(used)])
        item.start()
        used.append(item)
        return item

    wanted = [copy(query_at.at[:, pl.ds(base * 128, early)], query)]
    wanted.append(copy(first_at, first_in))
    wanted.append(copy(own_at, tiles.at[0]))
    wanted.append(copy(spot_at, spot))
    if last:
        for n in range(3):
            wanted.append(copy(ids_at[n].at[pl.ds(id_row, 16), :], tiles.at[n + 1]))
    loads = [[copy(moved_at[n], kv.at[n])] for n in range(3)]
    for half in range(2):
        here = pl.ds(half * (width // 2) + base * 128, early)
        loads.append([copy(cache_at.at[me, :, here], own.at[half])])
    later = [copy(update_at.at[:, pl.ds(base * 128, early)], update)]
    if last:
        later += [copy(cand_at.at[:, pl.ds(base * 128, early)], cand), copy(square_at, square)]
    for item in wanted:
        item.wait()
    if not last:
        for n in range(3):
            loads[n][0].wait()
            tiles[n + 1] = kv[n, pl.ds(id_row, 16), :]
        loads = loads[3:]
    first = first_in[...].astype(F32) > 0.5
    length_a = hist_ref[0].astype(F32)
    length_b = hist_ref[1].astype(F32)
    blocks = []
    masks = []
    for owner in range(owners):
        tile = tiles[owner].astype(F32)
        block_a, block_b = tile[0:1, :], tile[1:2, :]
        blocks.append((block_a, block_b))
        mask_a = jnp.where(first, jnp.where(block_a < length_a, 1.0, 0.0), 0.0)
        mask_b = jnp.where(first, 0.0, jnp.where(block_b < length_b, 1.0, 0.0))
        masks += [mask_a.astype(BF16), mask_b.astype(BF16)]
    mask = jnp.concatenate(masks, axis=1)
    place[...] = place_of(spot[0:1, :], place.shape[0])
    total = None
    stores = []
    for load in loads:
        for item in load:
            item.wait()
    for item in later:
        item.wait()
    for head in range(heads):
        cols = pl.ds(head * 128, 128)
        at_key, at_value = pl.ds(head * keys, keys), pl.ds((heads + head) * keys, keys)
        key = jnp.concatenate([own[0, :, cols]] + [kv[n, at_key, :] for n in range(3)], axis=0)
        value = jnp.concatenate([own[1, :, cols]] + [kv[n, at_value, :] for n in range(3)], axis=0)
        found = attend_head(base + head, first, mask, query[:, cols], key, value, blocks, bias_ref)
        total = found * found if total is None else total + found * found
        if last:
            attended[:, cols] = found * update[:, cols]
            continue
        stuff[:, cols] = (found * update[:, cols]).astype(BF16)
        if head % 2 == 1 or head == heads - 1:
            here = pl.ds(head // 2 * 256, 256 if head % 2 else 128)
            out[:, here] = jnp.dot(place[...], stuff[:, here], preferred_element_type=F32).astype(BF16)
            stores.append(copy(out.at[:, here], out_at.at[:, here]))
    if not last:
        square[...] = total
        stores.append(copy(stuff, stuff_at))
        stores.append(copy(square, square_at))
        for item in stores:
            item.wait()
        return
    feature = width // 2
    mean = jnp.sum(total + square[...], axis=1, keepdims=True) * (1.0 / feature)
    inv_rms = lax.rsqrt(mean + EPSILON)
    peers = out.shape[0]
    share = place.shape[0] // peers
    for i in range((heads + 1) // 2):
        some = min(2, heads - 2 * i)
        cols = pl.ds(i * 256, some * 128)
        block = (cand[:, cols].astype(F32) + attended[:, cols] * inv_rms).astype(BF16)
        stuff[:, cols] = block
        sent = jnp.dot(place[...], block, preferred_element_type=F32).astype(BF16)
        for j in range(some):
            here = pl.ds((2 * i + j) * share, share)
            out[:, here, :] = sent[:, j * 128 : (j + 1) * 128].reshape(peers, share, 128)
    scale = jnp.transpose(jnp.broadcast_to(inv_rms, (rows, 128)))[0:16, :]
    high = scale.astype(BF16).astype(F32)
    row = lax.broadcasted_iota(jnp.int32, scale.shape, 0)
    scale = jnp.where(row == 0, high, jnp.where(row == 1, scale - high, 0.0)).astype(BF16)
    scale = lax.dot_general(scale, place[...], NT, preferred_element_type=F32)
    each = 128 // share
    for peer in range(peers):
        tile = scale[:, (peer // each) * 128 : (peer // each + 1) * 128]
        if peer % each:
            tile = pltpu.roll(tile, 128 - (peer % each) * share, 1)
        out[peer, pl.ds(heads * share, 16), :] = tile.astype(BF16)
    stores.append(copy(out, out_at))
    square[...] = jnp.broadcast_to(inv_rms, square.shape)
    stores.append(copy(stuff, mixed_at))
    stores.append(copy(square, scale_at))
    for item in stores:
        item.wait()


def gate_kernel(tasks, ids_ref, weight_ref, cand_ref, stuff_ref, late_ref, scale_ref, out_ref):
    rows, early = stuff_ref.shape
    experts = weight_ref.shape[0] // tasks
    mixed = cand_ref[:, :early].astype(F32) + stuff_ref[...].astype(F32) * scale_ref[:, 0:1]
    logits = lax.dot_general(weight_ref[:, :early], mixed.astype(BF16), NT, preferred_element_type=F32)
    logits += lax.dot_general(weight_ref[:, early:], late_ref[...], NT, preferred_element_type=F32)
    squashed = []
    for k in range(2):
        hot = lax.broadcasted_iota(jnp.int32, (experts, rows), 0) == ids_ref[k : k + 1, :]
        picked = []
        for task in range(8):
            if task < tasks:
                here = logits[task * experts : (task + 1) * experts, :]
                picked.append(jnp.sum(jnp.where(hot, here, 0.0), axis=0, keepdims=True))
            else:
                picked.append(jnp.zeros((1, rows), F32))
        squashed.append(jax.nn.sigmoid(jnp.concatenate(picked, axis=0)))
    whole = squashed[0] + squashed[1]
    for k in range(2):
        out_ref[:, pl.ds(k * rows, rows)] = squashed[k] / whole


def early_kernel(cand_at, stuff_at, up_at, cand_out_at, stuff_out_at, rows, up, turned, out, sems):
    _, peers, share, early = rows.shape
    count, _, tile = up.shape
    used = []

    def copy(source, target):
        item = pltpu.make_async_copy(source, target, sems.at[len(used)])
        used.append(item)
        return item

    fetch = [copy(cand_at, rows.at[0]), copy(stuff_at, rows.at[1])]
    ups = []
    for i in range(count):
        here = pl.ds(i * tile, tile)
        ups.append(copy(up_at.at[0, pl.ds(0, early), here], up.at[i]))
    fetch[0].start()
    ups[0].start()
    fetch[1].start()
    stores = []
    for k, out_at in enumerate((cand_out_at, stuff_out_at)):
        fetch[k].wait()
        for i in range(early // 128):
            cols = pl.ds(i * 128, 128)
            block = rows[k, :, :, cols].reshape(peers * share, 128)
            turned[k, cols, :] = jnp.transpose(block * jnp.asarray(0.5, BF16))
        for i in range(count):
            if k == 0:
                ups[i].wait()
                if i + 1 < count:
                    ups[i + 1].start()
            found = lax.dot_general(up[i], turned[k], TN, preferred_element_type=F32)
            out[k, i] = found.astype(BF16)
            store = copy(out.at[k, i], out_at.at[pl.ds(i * tile, tile), :])
            store.start()
            stores.append(store)
    for store in stores:
        store.wait()


def expert_kernel(
    last_at, cand_product_at, stuff_product_at, up_at, tower_at, out_ref,
    last, cand_product, stuff_product, up, tower, turned, scale, sems,
):
    count, late, tile = up.shape
    early = up_at.shape[1] - late
    peers = last.shape[0]
    share = (last.shape[1] - 16) // (late // 128)
    rows = peers * share
    each = 128 // share
    fetch = pltpu.make_async_copy(last_at, last, sems.at[0])
    fetch.start()
    fetch_tower = pltpu.make_async_copy(tower_at, tower, sems.at[1])
    fetch_tower.start()
    loads = []
    for i in range(count):
        here = pl.ds(i * tile, tile)
        loads.append(
            (
                pltpu.make_async_copy(up_at.at[0, pl.ds(early, late), here], up.at[i], sems.at[3 * i + 2]),
                pltpu.make_async_copy(cand_product_at.at[here, :], cand_product.at[i], sems.at[3 * i + 3]),
                pltpu.make_async_copy(stuff_product_at.at[here, :], stuff_product.at[i], sems.at[3 * i + 4]),
            )
        )
    for item in loads[0]:
        item.start()
    fetch.wait()
    for ahead in range(1, AHEAD):
        for item in loads[ahead]:
            item.start()
    lane = lax.broadcasted_iota(jnp.int32, (16, 128), 1)
    for group in range(peers // each):
        whole_tile = None
        for i in range(each):
            part = last[group * each + i, pl.ds(late // 128 * share, 16), :].astype(F32)
            part = pltpu.roll(part, i * share, 1) if i else part
            part = jnp.where((lane >= i * share) & (lane < (i + 1) * share), part, 0.0)
            whole_tile = part if whole_tile is None else whole_tile + part
        scale[:, pl.ds(group * 128, 128)] = whole_tile[0:1, :] + whole_tile[1:2, :]
    for i in range(late // 128):
        block = last[:, pl.ds(i * share, share), :].reshape(rows, 128)
        turned[pl.ds(i * 128, 128), :] = jnp.transpose(block * jnp.asarray(0.5, BF16))
    fetch_tower.wait()
    total = None
    row_scale = scale[...].astype(BF16)
    for i in range(count):
        if i + AHEAD < count:
            for item in loads[i + AHEAD]:
                item.start()
        for item in loads[i]:
            item.wait()
        half = lax.dot_general(up[i], turned[...], TN, preferred_element_type=F32)
        half = half + (cand_product[i] + stuff_product[i] * row_scale).astype(F32)
        hidden = (half + half * jnp.tanh(half)).astype(BF16)
        part = jnp.dot(tower[:, pl.ds(i * tile, tile)], hidden, preferred_element_type=F32)
        total = part if total is None else total + part
    found = total[0:8, :] + total[8:16, :]
    for peer in range(peers):
        out_ref[peer] = found[:, (peer // each) * 128 : (peer // each + 1) * 128]


def combine_kernel(capacity, lane_ref, spot_ref, ids_ref, gate_ref, back_ref, out_ref):
    rows = ids_ref.shape[1]
    experts = back_ref.shape[0] // 8
    ids = jnp.concatenate([ids_ref[0:1, :], ids_ref[1:2, :]], axis=1)
    lane = spot_ref[0:1, :] - ids * capacity + lane_ref[0]
    hot = lax.broadcasted_iota(jnp.int32, (128, 2 * rows), 0) == lane
    hot = jnp.where(hot, 1.0, 0.0).astype(BF16)
    back = back_ref[...]
    high = back.astype(BF16)
    rest = back - high.astype(F32)
    middle = rest.astype(BF16)
    low = (rest - middle.astype(F32)).astype(BF16)
    found = jnp.dot(high, hot, preferred_element_type=F32)
    found += jnp.dot(middle, hot, preferred_element_type=F32)
    found += jnp.dot(low, hot, preferred_element_type=F32)
    total = jnp.zeros((8, 2 * rows), F32)
    for expert in range(experts):
        total = jnp.where(ids == expert, found[expert * 8 : (expert + 1) * 8], total)
    total = total * gate_ref[...]
    total = total[:, :rows] + total[:, rows:]
    out_ref[...] = total[: out_ref.shape[0]]


def params(mib=63):
    return pltpu.CompilerParams(vmem_limit_bytes=mib * 2**20)


def cost(flops, bytes_accessed, transcendentals=0):
    return pl.CostEstimate(flops=flops, bytes_accessed=bytes_accessed, transcendentals=transcendentals)


def whole(*shape):
    return pl.BlockSpec(shape, lambda i, *_: (0,) * len(shape))


def local(
    cand_emb,
    cand_request,
    hist_blocks,
    cache_kv,
    block_map,
    w_query_update,
    rel_bias,
    norm_gain,
    w_gate,
    expert_ids,
    w_up,
    w_down,
    w_tower,
):
    rows, feature = cand_emb.shape
    owners = lax.axis_size("req")
    me = lax.axis_index("req").astype(jnp.int32)
    head_count = rel_bias.shape[0]
    tasks = w_tower.shape[1]
    experts = w_gate.shape[1] // tasks
    capacity = 2 * rows * expert_ids.shape[1] // experts
    slots = experts * capacity
    chunk_heads = (HEADS_FIRST, head_count - HEADS_FIRST)
    early = HEADS_FIRST * 128
    keys = cache_kv.shape[0] // owners * cache_kv.shape[1]
    me_scalar = me[None]
    smem = pl.BlockSpec(memory_space=pltpu.SMEM)
    anywhere = pl.BlockSpec(memory_space=pl.ANY)
    hbm = pl.BlockSpec(memory_space=pltpu.HBM)

    cache = cache_kv.reshape(owners, keys, 2 * feature)

    def pack(chunk):
        parts = 2 * chunk_heads[chunk]
        tail = 16 if chunk == 0 else 0
        shapes = [jax.ShapeDtypeStruct((parts * keys + tail, 128), BF16)] * len(SHIFTS)
        specs = [anywhere] * len(SHIFTS)
        if chunk == 0:
            shapes.append(jax.ShapeDtypeStruct((16, 128), BF16))
            specs.append(pl.BlockSpec(memory_space=pltpu.VMEM))
        return pl.pallas_call(
            functools.partial(pack_kernel, chunk),
            in_specs=[smem, smem, anywhere],
            out_specs=specs,
            out_shape=shapes,
            scratch_shapes=[
                pltpu.VMEM((len(SHIFTS), parts * keys + tail, 128), BF16),
                pltpu.SemaphoreType.DMA((2, len(SHIFTS), parts + 1)),
            ],
            compiler_params=params(),
            cost_estimate=cost(0, 10**6),
            name="pack",
        )(me_scalar, block_map, cache)

    def send(item, shift):
        pairs = [(i, (i + shift) % owners) for i in range(owners)]
        return lax.ppermute(item, "req", pairs)

    *packed, own_tile = pack(0)
    first_moved = [send(item, shift) for item, shift in zip(packed, SHIFTS)]
    packed_last = pack(1)
    last_moved = []
    for item, ahead, shift in zip(packed_last, first_moved, SHIFTS):
        item, _ = lax.optimization_barrier((item, ahead))
        last_moved.append(send(item, shift))

    ids_rows, _ = lax.optimization_barrier((expert_ids.T, own_tile))
    each = 128 // capacity
    lane = lax.rem(lax.axis_index("exp").astype(jnp.int32), each) * capacity
    spots, first, cand_out = pl.pallas_call(
        functools.partial(route_kernel, capacity),
        grid=(1,),
        in_specs=[
            whole(2, rows),
            whole(1, rows),
            pl.BlockSpec((rows, early), lambda i: (0, 0)),
        ],
        out_specs=[whole(8, 2 * rows), whole(rows, 128), whole(slots, early)],
        out_shape=[
            jax.ShapeDtypeStruct((8, 2 * rows), jnp.int32),
            jax.ShapeDtypeStruct((rows, 128), BF16),
            jax.ShapeDtypeStruct((slots, early), BF16),
        ],
        compiler_params=params(),
        cost_estimate=cost(5 * 10**8, 3 * 10**6),
        name="route",
    )(ids_rows, cand_request[None, :], cand_emb)

    def exchange(item):
        return lax.all_to_all(item, "exp", split_axis=0, concat_axis=0, tiled=True)

    cand_in = exchange(cand_out.reshape(experts, capacity, early))

    cand_rows, _, _ = lax.optimization_barrier((cand_emb, spots, packed_last[0]))
    steps = 4
    wide = 2 * feature // steps
    queries, update = pl.pallas_call(
        project_kernel,
        in_specs=[
            pl.BlockSpec(memory_space=pltpu.VMEM),
            anywhere,
            pl.BlockSpec(memory_space=pltpu.VMEM),
        ],
        out_shape=[
            jax.ShapeDtypeStruct((rows, feature), BF16),
            jax.ShapeDtypeStruct((rows, feature), F32),
        ],
        scratch_shapes=[pltpu.VMEM((steps, feature, wide), BF16), pltpu.SemaphoreType.DMA((steps,))],
        compiler_params=params(),
        cost_estimate=cost(11 * 10**8, 6 * 10**6, 2**18),
        name="project",
    )(cand_rows, w_query_update, norm_gain[None, :])

    hidden_count = w_up.shape[2]
    tile = 512
    def attend(chunk, moved, extra, out_shape, extra_scratch, name, flops):
        arrays = [queries, cache, *moved, *first_moved, own_tile, first, update, spots, *extra]
        out_rows = out_shape[0].shape
        parts = 2 * chunk_heads[chunk]
        wide = parts * 64
        return pl.pallas_call(
            functools.partial(attend_kernel, chunk),
            in_specs=[smem] * 3 + [anywhere] * len(arrays),
            out_specs=[anywhere] * len(out_shape),
            out_shape=out_shape,
            scratch_shapes=[
                pltpu.SemaphoreType.DMA((16 + 4 * parts,)),
                pltpu.VMEM((owners - 1, *moved[0].shape), BF16),
                pltpu.VMEM((2, keys, wide), BF16),
                pltpu.VMEM((owners, 16, 128), BF16),
                pltpu.VMEM((rows, wide), BF16),
                pltpu.VMEM((rows, 128), BF16),
                pltpu.VMEM((rows, wide), F32),
                pltpu.VMEM((8, 2 * rows), jnp.int32),
                pltpu.VMEM((slots, rows), BF16),
                pltpu.VMEM((rows, 128), F32),
                pltpu.VMEM((rows, wide), BF16),
                pltpu.VMEM(out_rows, BF16),
                *extra_scratch,
            ],
            compiler_params=params(),
            cost_estimate=cost(flops, 10**6),
            name=name,
        )(me_scalar, hist_blocks, rel_bias.T, *arrays)

    stuff_out, stuff, square = attend(
        0,
        first_moved,
        [],
        [
            jax.ShapeDtypeStruct((slots, early), BF16),
            jax.ShapeDtypeStruct((rows, early), BF16),
            jax.ShapeDtypeStruct((rows, 128), F32),
        ],
        [],
        "attend_first",
        FIRST_COST,
    )
    stuff_in = exchange(stuff_out.reshape(experts, capacity, early))

    tower_rows = jnp.pad(w_tower.T, ((0, 16 - tasks), (0, 0)))
    tower_rows, _ = lax.optimization_barrier((tower_rows, cand_in))
    towers = pl.pallas_call(
        tower_kernel,
        in_specs=[pl.BlockSpec(memory_space=pl.ANY), pl.BlockSpec(memory_space=pltpu.VMEM)],
        out_shape=jax.ShapeDtypeStruct((16, hidden_count), BF16),
        scratch_shapes=[
            pltpu.VMEM((hidden_count // tile, tile, feature), BF16),
            pltpu.SemaphoreType.DMA((hidden_count // tile,)),
        ],
        compiler_params=params(),
        cost_estimate=cost(10**8, 9 * 10**6),
        name="tower",
    )(w_down, tower_rows)


    square, _ = lax.optimization_barrier((square, towers))
    last_rows = chunk_heads[1] * capacity + 16
    late = feature - early
    last_out, late_mixed, row_scale = attend(
        1,
        last_moved,
        [cand_emb, square],
        [
            jax.ShapeDtypeStruct((experts, last_rows, 128), BF16),
            jax.ShapeDtypeStruct((rows, late), BF16),
            jax.ShapeDtypeStruct((rows, 128), F32),
        ],
        [pltpu.VMEM((rows, late), BF16), pltpu.VMEM((rows, late), F32)],
        "attend_last",
        LAST_COST,
    )
    last_in = exchange(last_out)
    wide = hidden_count // 4
    products = [jax.ShapeDtypeStruct((hidden_count, slots), BF16)] * 2
    cand_product, stuff_product = pl.pallas_call(
        early_kernel,
        in_specs=[anywhere] * 3,
        out_specs=[anywhere] * 2,
        out_shape=products,
        scratch_shapes=[
            pltpu.VMEM((2, experts, capacity, early), BF16),
            pltpu.VMEM((4, early, wide), BF16),
            pltpu.VMEM((2, early, slots), BF16),
            pltpu.VMEM((2, 4, wide, slots), BF16),
            pltpu.SemaphoreType.DMA((16,)),
        ],
        compiler_params=params(),
        cost_estimate=cost(EARLY_COST, 10**6),
        name="early",
    )(cand_in, stuff_in, w_up)

    gates = pl.pallas_call(
        functools.partial(gate_kernel, tasks),
        out_shape=jax.ShapeDtypeStruct((8, 2 * rows), F32),
        compiler_params=params(GATE_LIMIT),
        cost_estimate=cost(10**8, 2 * 10**6, 4096),
        name="gate",
    )(ids_rows, w_gate.T, cand_emb, stuff, late_mixed, row_scale)

    late = feature - early
    count = hidden_count // tile
    produced = pl.pallas_call(
        expert_kernel,
        in_specs=[anywhere] * 5,
        out_shape=jax.ShapeDtypeStruct((experts, 8, 128), F32),
        scratch_shapes=[
            pltpu.VMEM((experts, last_rows, 128), BF16),
            pltpu.VMEM((count, tile, slots), BF16),
            pltpu.VMEM((count, tile, slots), BF16),
            pltpu.VMEM((count, late, tile), BF16),
            pltpu.VMEM((16, hidden_count), BF16),
            pltpu.VMEM((late, slots), BF16),
            pltpu.VMEM((1, slots), F32),
            pltpu.SemaphoreType.DMA((3 * count + 2,)),
        ],
        compiler_params=params(),
        cost_estimate=cost(6 * 10**9, 25 * 10**6, 2**22),
        name="expert",
    )(last_in, cand_product, stuff_product, w_up, towers)

    came_back = exchange(produced)

    vmem = pl.BlockSpec(memory_space=pltpu.VMEM)
    scores = pl.pallas_call(
        functools.partial(combine_kernel, capacity),
        in_specs=[smem, vmem, vmem, vmem, vmem],
        out_shape=jax.ShapeDtypeStruct((tasks, rows), F32),
        compiler_params=params(COMBINE_LIMIT),
        cost_estimate=cost(10**8, 10**6),
        name="combine",
    )(lane[None], spots, ids_rows, gates, came_back.reshape(experts * 8, 128))
    return scores.T


def solution(mesh):
    placed = (
        P(("req", "exp"), None),
        P(("req", "exp")),
        P(("req", "exp")),
        P(("req", "exp"), None, None),
        P(("req", "exp")),
        P(),
        P(),
        P(),
        P(),
        P(("req", "exp"), None),
        P("exp", None, None),
        P("exp", None, None),
        P(),
    )
    return jax.shard_map(
        local, mesh=mesh, in_specs=placed, out_specs=P(("req", "exp"), None), check_vma=False
    )
```

```python
import functools
import math

import jax
import jax.numpy as jnp
from jax import lax
from jax.experimental import pallas as pl
from jax.experimental.pallas import tpu as pltpu
from jax.sharding import PartitionSpec as P

EPSILON = 1e-05
F32 = jnp.float32
BF16 = jnp.bfloat16
NT = (((1,), (1,)), ((), ()))
TN = (((0,), (0,)), ((), ()))
SHIFTS = (1, 3, 2)
HEADS_FIRST = 4
GATE_LIMIT = 8
COMBINE_LIMIT = 8
AHEAD = 3
FIRST_COST = 30 * 10**9
EARLY_COST = 5 * 10**9
LAST_COST = 100 * 10**9


def pack_kernel(chunk, me_ref, ids_ref, cache_at, *refs):
    count = len(SHIFTS)
    packed, sems = refs[-2:]
    outs = refs[:-2]
    owners, keys, width = cache_at.shape
    parts = packed.shape[1] // keys
    heads = parts // 2
    first = chunk * (width // 256 - heads)
    me = me_ref[0]
    loads = []
    for n, shift in enumerate(SHIFTS):
        to = lax.rem(me + shift, owners)
        for part in range(parts):
            col = (first + part % heads) * 128 + (part // heads) * (width // 2)
            here = packed.at[n, pl.ds(part * keys, keys), :]
            load = pltpu.make_async_copy(cache_at.at[to, :, pl.ds(col, 128)], here, sems.at[0, n, part])
            load.start()
            store = pltpu.make_async_copy(here, outs[n].at[pl.ds(part * keys, keys), :], sems.at[1, n, part])
            loads.append((load, store))
    stores = []
    if len(outs) > count:
        row = lax.broadcasted_iota(jnp.int32, (16, 128), 0)

        def tile_of(owner):
            one = ids_ref[2 * owner].astype(F32)
            two = ids_ref[2 * owner + 1].astype(F32)
            return jnp.where(row == 0, one, two).astype(BF16)

        for n, shift in enumerate(SHIFTS):
            here = pl.ds(parts * keys, 16)
            packed[n, here, :] = tile_of(lax.rem(me + shift, owners))
            store = pltpu.make_async_copy(packed.at[n, here, :], outs[n].at[here, :], sems.at[1, n, parts])
            store.start()
            stores.append(store)
        outs[count][...] = tile_of(me)
    for load, store in loads:
        load.wait()
        store.start()
        stores.append(store)
    for store in stores:
        store.wait()


def place_of(slot, slots):
    rows = slot.shape[1] // 2
    spot = lax.broadcasted_iota(jnp.int32, (slots, rows), 0)
    place = (spot == slot[:, :rows]) | (spot == slot[:, rows:])
    return jnp.where(place, 1.0, 0.0).astype(BF16)


def route_kernel(capacity, ids_ref, req_ref, cand_ref, spot_ref, first_ref, out_ref):
    rows = ids_ref.shape[1]
    experts = out_ref.shape[0] // capacity
    ids = jnp.concatenate([ids_ref[0:1, :], ids_ref[1:2, :]], axis=1)
    hot = lax.broadcasted_iota(jnp.int32, (experts, 2 * rows), 0) == ids
    hot = jnp.where(hot, 1.0, 0.0)
    here = lax.broadcasted_iota(jnp.int32, (2 * rows, 2 * rows), 0)
    there = lax.broadcasted_iota(jnp.int32, (2 * rows, 2 * rows), 1)
    earlier = jnp.where(here < there, 1.0, 0.0).astype(BF16)
    counts = jnp.dot(hot.astype(BF16), earlier, preferred_element_type=F32)
    position = jnp.sum(counts * hot, axis=0, keepdims=True).astype(jnp.int32)
    slot = ids * capacity + position
    spot_ref[...] = jnp.broadcast_to(slot, spot_ref.shape)
    place = place_of(slot, out_ref.shape[0])
    out_ref[...] = jnp.dot(place, cand_ref[...], preferred_element_type=F32).astype(BF16)
    first = jnp.where(req_ref[...] == 0, 1.0, 0.0)
    first_ref[...] = jnp.transpose(jnp.broadcast_to(first, (128, rows))).astype(BF16)


def project_kernel(cand_ref, weight_at, gain_ref, query_ref, update_ref, weight, sems):
    count, _, wide = weight.shape
    loads = []
    for i in range(count):
        here = pl.ds(i * wide, wide)
        loads.append(pltpu.make_async_copy(weight_at.at[:, here], weight.at[i], sems.at[i]))
        loads[i].start()
    for i in range(count):
        loads[i].wait()
        projected = jnp.dot(cand_ref[...], weight[i], preferred_element_type=F32)
        cols = pl.ds(i % (count // 2) * wide, wide)
        if i < count // 2:
            query_ref[:, cols] = projected.astype(BF16)
        else:
            update_ref[:, cols] = gain_ref[:, cols] * projected / (1.0 + jnp.exp(-projected))


def tower_kernel(down_at, tower_ref, out_ref, down, sems):
    count, tile, _ = down.shape
    loads = []
    for i in range(count):
        here = pl.ds(i * tile, tile)
        loads.append(pltpu.make_async_copy(down_at.at[0, here, :], down.at[i], sems.at[i]))
    for i in range(2):
        loads[i].start()
    for i in range(count):
        if i + 2 < count:
            loads[i + 2].start()
        loads[i].wait()
        product = lax.dot_general(tower_ref[...], down[i], NT, preferred_element_type=F32)
        high = product.astype(BF16)
        low = (product - high.astype(F32)).astype(BF16)
        out_ref[:, pl.ds(i * tile, tile)] = jnp.concatenate([high[0:8], low[0:8]], axis=0)


def attend_head(head, first, mask, query, key, value, blocks, bias_ref):
    scores = lax.dot_general(query, key, NT, preferred_element_type=F32)
    weights = []
    for owner, (block_a, block_b) in enumerate(blocks):
        here = scores[:, owner * 256 : (owner + 1) * 256]
        here = jnp.where(first, here[:, :128], here[:, 128:])
        bias_a = jnp.zeros_like(block_a)
        bias_b = jnp.zeros_like(block_b)
        for block in range(bias_ref.shape[0]):
            entry = bias_ref[block, head] * 0.5
            bias_a = jnp.where(block_a == block, entry, bias_a)
            bias_b = jnp.where(block_b == block, entry, bias_b)
        half = here * (0.5 / math.sqrt(128.0)) + jnp.where(first, bias_a, bias_b)
        weight = (half + half * jnp.tanh(half)).astype(BF16)
        weights += [weight, weight]
    weights = jnp.concatenate(weights, axis=1) * mask
    return jnp.dot(weights, value, preferred_element_type=F32)


def attend_kernel(chunk, me_ref, hist_ref, bias_ref, *refs):
    last = chunk == 1
    query_at, cache_at, *refs = refs
    moved_at, refs = refs[:3], refs[3:]
    ids_at, refs = refs[:3], refs[3:]
    own_at, first_at, update_at, spot_at, *refs = refs
    if last:
        cand_at, square_at, *refs = refs
        out_at, mixed_at, scale_at, *refs = refs
    else:
        out_at, stuff_at, square_at, *refs = refs
    sems, kv, own, tiles, query, first_in, update, spot, place, square, stuff, out, *refs = refs
    if last:
        cand, attended = refs
    owners, keys, width = cache_at.shape
    heads = own.shape[2] // 128
    early = heads * 128
    base = chunk * (width // 256 - heads)
    id_row = ids_at[0].shape[0] - 16
    rows = query.shape[0]
    me = me_ref[0]
    used = []

    def copy(source, target):
        item = pltpu.make_async_copy(source, target, sems.at[len(used)])
        item.start()
        used.append(item)
        return item

    wanted = [copy(query_at.at[:, pl.ds(base * 128, early)], query)]
    wanted.append(copy(first_at, first_in))
    wanted.append(copy(own_at, tiles.at[0]))
    wanted.append(copy(spot_at, spot))
    if last:
        for n in range(3):
            wanted.append(copy(ids_at[n].at[pl.ds(id_row, 16), :], tiles.at[n + 1]))
    loads = [[copy(moved_at[n], kv.at[n])] for n in range(3)]
    for half in range(2):
        here = pl.ds(half * (width // 2) + base * 128, early)
        loads.append([copy(cache_at.at[me, :, here], own.at[half])])
    later = [copy(update_at.at[:, pl.ds(base * 128, early)], update)]
    if last:
        later += [copy(cand_at.at[:, pl.ds(base * 128, early)], cand), copy(square_at, square)]
    for item in wanted:
        item.wait()
    if not last:
        for n in range(3):
            loads[n][0].wait()
            tiles[n + 1] = kv[n, pl.ds(id_row, 16), :]
        loads = loads[3:]
    first = first_in[...].astype(F32) > 0.5
    length_a = hist_ref[0].astype(F32)
    length_b = hist_ref[1].astype(F32)
    blocks = []
    masks = []
    for owner in range(owners):
        tile = tiles[owner].astype(F32)
        block_a, block_b = tile[0:1, :], tile[1:2, :]
        blocks.append((block_a, block_b))
        mask_a = jnp.where(first, jnp.where(block_a < length_a, 1.0, 0.0), 0.0)
        mask_b = jnp.where(first, 0.0, jnp.where(block_b < length_b, 1.0, 0.0))
        masks += [mask_a.astype(BF16), mask_b.astype(BF16)]
    mask = jnp.concatenate(masks, axis=1)
    place[...] = place_of(spot[0:1, :], place.shape[0])
    total = None
    stores = []
    for load in loads:
        for item in load:
            item.wait()
    for item in later:
        item.wait()
    for head in range(heads):
        cols = pl.ds(head * 128, 128)
        at_key, at_value = pl.ds(head * keys, keys), pl.ds((heads + head) * keys, keys)
        key = jnp.concatenate([own[0, :, cols]] + [kv[n, at_key, :] for n in range(3)], axis=0)
        value = jnp.concatenate([own[1, :, cols]] + [kv[n, at_value, :] for n in range(3)], axis=0)
        found = attend_head(base + head, first, mask, query[:, cols], key, value, blocks, bias_ref)
        total = found * found if total is None else total + found * found
        if last:
            attended[:, cols] = found * update[:, cols]
            continue
        stuff[:, cols] = (found * update[:, cols]).astype(BF16)
        if head % 2 == 1 or head == heads - 1:
            here = pl.ds(head // 2 * 256, 256 if head % 2 else 128)
            out[:, here] = jnp.dot(place[...], stuff[:, here], preferred_element_type=F32).astype(BF16)
            stores.append(copy(out.at[:, here], out_at.at[:, here]))
    if not last:
        square[...] = total
        stores.append(copy(stuff, stuff_at))
        stores.append(copy(square, square_at))
        for item in stores:
            item.wait()
        return
    feature = width // 2
    mean = jnp.sum(total + square[...], axis=1, keepdims=True) * (1.0 / feature)
    inv_rms = lax.rsqrt(mean + EPSILON)
    peers = out.shape[0]
    share = place.shape[0] // peers
    for i in range((heads + 1) // 2):
        some = min(2, heads - 2 * i)
        cols = pl.ds(i * 256, some * 128)
        block = (cand[:, cols].astype(F32) + attended[:, cols] * inv_rms).astype(BF16)
        stuff[:, cols] = block
        sent = jnp.dot(place[...], block, preferred_element_type=F32).astype(BF16)
        for j in range(some):
            here = pl.ds((2 * i + j) * share, share)
            out[:, here, :] = sent[:, j * 128 : (j + 1) * 128].reshape(peers, share, 128)
    scale = jnp.transpose(jnp.broadcast_to(inv_rms, (rows, 128)))[0:16, :]
    high = scale.astype(BF16).astype(F32)
    row = lax.broadcasted_iota(jnp.int32, scale.shape, 0)
    scale = jnp.where(row == 0, high, jnp.where(row == 1, scale - high, 0.0)).astype(BF16)
    scale = lax.dot_general(scale, place[...], NT, preferred_element_type=F32)
    each = 128 // share
    for peer in range(peers):
        tile = scale[:, (peer // each) * 128 : (peer // each + 1) * 128]
        if peer % each:
            tile = pltpu.roll(tile, 128 - (peer % each) * share, 1)
        out[peer, pl.ds(heads * share, 16), :] = tile.astype(BF16)
    stores.append(copy(out, out_at))
    square[...] = jnp.broadcast_to(inv_rms, square.shape)
    stores.append(copy(stuff, mixed_at))
    stores.append(copy(square, scale_at))
    for item in stores:
        item.wait()


def gate_kernel(tasks, ids_ref, weight_ref, cand_ref, stuff_ref, late_ref, scale_ref, out_ref):
    rows, early = stuff_ref.shape
    experts = weight_ref.shape[0] // tasks
    mixed = cand_ref[:, :early].astype(F32) + stuff_ref[...].astype(F32) * scale_ref[:, 0:1]
    logits = lax.dot_general(weight_ref[:, :early], mixed.astype(BF16), NT, preferred_element_type=F32)
    logits += lax.dot_general(weight_ref[:, early:], late_ref[...], NT, preferred_element_type=F32)
    squashed = []
    for k in range(2):
        hot = lax.broadcasted_iota(jnp.int32, (experts, rows), 0) == ids_ref[k : k + 1, :]
        picked = []
        for task in range(8):
            if task < tasks:
                here = logits[task * experts : (task + 1) * experts, :]
                picked.append(jnp.sum(jnp.where(hot, here, 0.0), axis=0, keepdims=True))
            else:
                picked.append(jnp.zeros((1, rows), F32))
        squashed.append(jax.nn.sigmoid(jnp.concatenate(picked, axis=0)))
    whole = squashed[0] + squashed[1]
    for k in range(2):
        out_ref[:, pl.ds(k * rows, rows)] = squashed[k] / whole


def early_kernel(cand_at, stuff_at, up_at, cand_out_at, stuff_out_at, rows, up, turned, out, sems):
    _, peers, share, early = rows.shape
    count, _, tile = up.shape
    used = []

    def copy(source, target):
        item = pltpu.make_async_copy(source, target, sems.at[len(used)])
        used.append(item)
        return item

    fetch = [copy(cand_at, rows.at[0]), copy(stuff_at, rows.at[1])]
    ups = []
    for i in range(count):
        here = pl.ds(i * tile, tile)
        ups.append(copy(up_at.at[0, pl.ds(0, early), here], up.at[i]))
    fetch[0].start()
    ups[0].start()
    fetch[1].start()
    stores = []
    for k, out_at in enumerate((cand_out_at, stuff_out_at)):
        fetch[k].wait()
        for i in range(early // 128):
            cols = pl.ds(i * 128, 128)
            block = rows[k, :, :, cols].reshape(peers * share, 128)
            turned[k, cols, :] = jnp.transpose(block * jnp.asarray(0.5, BF16))
        for i in range(count):
            if k == 0:
                ups[i].wait()
                if i + 1 < count:
                    ups[i + 1].start()
            found = lax.dot_general(up[i], turned[k], TN, preferred_element_type=F32)
            out[k, i] = found.astype(BF16)
            store = copy(out.at[k, i], out_at.at[pl.ds(i * tile, tile), :])
            store.start()
            stores.append(store)
    for store in stores:
        store.wait()


def expert_kernel(
    last_at, cand_product_at, stuff_product_at, up_at, tower_at, out_ref,
    last, cand_product, stuff_product, up, tower, turned, scale, sems,
):
    count, late, tile = up.shape
    early = up_at.shape[1] - late
    peers = last.shape[0]
    share = (last.shape[1] - 16) // (late // 128)
    rows = peers * share
    each = 128 // share
    fetch = pltpu.make_async_copy(last_at, last, sems.at[0])
    fetch.start()
    fetch_tower = pltpu.make_async_copy(tower_at, tower, sems.at[1])
    fetch_tower.start()
    loads = []
    for i in range(count):
        here = pl.ds(i * tile, tile)
        loads.append(
            (
                pltpu.make_async_copy(up_at.at[0, pl.ds(early, late), here], up.at[i], sems.at[3 * i + 2]),
                pltpu.make_async_copy(cand_product_at.at[here, :], cand_product.at[i], sems.at[3 * i + 3]),
                pltpu.make_async_copy(stuff_product_at.at[here, :], stuff_product.at[i], sems.at[3 * i + 4]),
            )
        )
    for item in loads[0]:
        item.start()
    fetch.wait()
    for ahead in range(1, AHEAD):
        for item in loads[ahead]:
            item.start()
    lane = lax.broadcasted_iota(jnp.int32, (16, 128), 1)
    for group in range(peers // each):
        whole_tile = None
        for i in range(each):
            part = last[group * each + i, pl.ds(late // 128 * share, 16), :].astype(F32)
            part = pltpu.roll(part, i * share, 1) if i else part
            part = jnp.where((lane >= i * share) & (lane < (i + 1) * share), part, 0.0)
            whole_tile = part if whole_tile is None else whole_tile + part
        scale[:, pl.ds(group * 128, 128)] = whole_tile[0:1, :] + whole_tile[1:2, :]
    for i in range(late // 128):
        block = last[:, pl.ds(i * share, share), :].reshape(rows, 128)
        turned[pl.ds(i * 128, 128), :] = jnp.transpose(block * jnp.asarray(0.5, BF16))
    fetch_tower.wait()
    total = None
    row_scale = scale[...].astype(BF16)
    for i in range(count):
        if i + AHEAD < count:
            for item in loads[i + AHEAD]:
                item.start()
        for item in loads[i]:
            item.wait()
        half = lax.dot_general(up[i], turned[...], TN, preferred_element_type=F32)
        half = half + (cand_product[i] + stuff_product[i] * row_scale).astype(F32)
        hidden = (half + half * jnp.tanh(half)).astype(BF16)
        part = jnp.dot(tower[:, pl.ds(i * tile, tile)], hidden, preferred_element_type=F32)
        total = part if total is None else total + part
    found = total[0:8, :] + total[8:16, :]
    row = lax.broadcasted_iota(jnp.int32, (8, 128), 0)
    mine = lax.broadcasted_iota(jnp.int32, (8, 128), 1) // share == row % each
    for group in range(peers // each):
        tile = found[:, group * 128 : (group + 1) * 128]
        turns = [tile] + [pltpu.roll(tile, k * share, 1) for k in range(1, each)]
        for i in range(each):
            kept = jnp.zeros((8, 128), F32)
            for k in range(each):
                kept = jnp.where(mine & (row % each == (i + k) % each), turns[k], kept)
            rows_out = []
            for half in range(2):
                line = kept[half * 4 : half * 4 + 1]
                for j in range(1, 4):
                    line = line + kept[half * 4 + j : half * 4 + j + 1]
                rows_out.append(line)
            out_ref[group * each + i] = jnp.concatenate(rows_out, axis=0)


def combine_kernel(capacity, spot_ref, ids_ref, gate_ref, back_ref, out_ref):
    rows = ids_ref.shape[1]
    experts = back_ref.shape[0] // 2
    ids = jnp.concatenate([ids_ref[0:1, :], ids_ref[1:2, :]], axis=1)
    position = spot_ref[0:1, :] - ids * capacity
    back = back_ref[...]
    high = back.astype(BF16)
    rest = back - high.astype(F32)
    middle = rest.astype(BF16)
    low = (rest - middle.astype(F32)).astype(BF16)
    lanes = lax.broadcasted_iota(jnp.int32, (128, 2 * rows), 0)
    picked = []
    for task in range(128 // capacity):
        hot = jnp.where(lanes == position + task * capacity, 1.0, 0.0).astype(BF16)
        found = jnp.dot(high, hot, preferred_element_type=F32)
        found += jnp.dot(middle, hot, preferred_element_type=F32)
        found += jnp.dot(low, hot, preferred_element_type=F32)
        total = jnp.zeros((8, 2 * rows), F32)
        for group in range(experts // 4):
            owner = group * 4 + lax.broadcasted_iota(jnp.int32, (8, 2 * rows), 0) // 2
            total = total + jnp.where(ids == owner, found[group * 8 : (group + 1) * 8], 0.0)
        picked.append(total)
    lines = []
    for half in range(2):
        for total in picked:
            line = total[half : half + 1]
            for pair in range(1, 4):
                line = line + total[2 * pair + half : 2 * pair + half + 1]
            lines.append(line)
    total = jnp.concatenate(lines, axis=0) * gate_ref[...]
    total = total[:, :rows] + total[:, rows:]
    out_ref[...] = total[: out_ref.shape[0]]


def params(mib=63):
    return pltpu.CompilerParams(vmem_limit_bytes=mib * 2**20)


def cost(flops, bytes_accessed, transcendentals=0):
    return pl.CostEstimate(flops=flops, bytes_accessed=bytes_accessed, transcendentals=transcendentals)


def whole(*shape):
    return pl.BlockSpec(shape, lambda i, *_: (0,) * len(shape))


def local(
    cand_emb,
    cand_request,
    hist_blocks,
    cache_kv,
    block_map,
    w_query_update,
    rel_bias,
    norm_gain,
    w_gate,
    expert_ids,
    w_up,
    w_down,
    w_tower,
):
    rows, feature = cand_emb.shape
    owners = lax.axis_size("req")
    me = lax.axis_index("req").astype(jnp.int32)
    head_count = rel_bias.shape[0]
    tasks = w_tower.shape[1]
    experts = w_gate.shape[1] // tasks
    capacity = 2 * rows * expert_ids.shape[1] // experts
    slots = experts * capacity
    chunk_heads = (HEADS_FIRST, head_count - HEADS_FIRST)
    early = HEADS_FIRST * 128
    keys = cache_kv.shape[0] // owners * cache_kv.shape[1]
    me_scalar = me[None]
    smem = pl.BlockSpec(memory_space=pltpu.SMEM)
    anywhere = pl.BlockSpec(memory_space=pl.ANY)
    hbm = pl.BlockSpec(memory_space=pltpu.HBM)

    cache = cache_kv.reshape(owners, keys, 2 * feature)

    def pack(chunk):
        parts = 2 * chunk_heads[chunk]
        tail = 16 if chunk == 0 else 0
        shapes = [jax.ShapeDtypeStruct((parts * keys + tail, 128), BF16)] * len(SHIFTS)
        specs = [anywhere] * len(SHIFTS)
        if chunk == 0:
            shapes.append(jax.ShapeDtypeStruct((16, 128), BF16))
            specs.append(pl.BlockSpec(memory_space=pltpu.VMEM))
        return pl.pallas_call(
            functools.partial(pack_kernel, chunk),
            in_specs=[smem, smem, anywhere],
            out_specs=specs,
            out_shape=shapes,
            scratch_shapes=[
                pltpu.VMEM((len(SHIFTS), parts * keys + tail, 128), BF16),
                pltpu.SemaphoreType.DMA((2, len(SHIFTS), parts + 1)),
            ],
            compiler_params=params(),
            cost_estimate=cost(0, 10**6),
            name="pack",
        )(me_scalar, block_map, cache)

    def send(item, shift):
        pairs = [(i, (i + shift) % owners) for i in range(owners)]
        return lax.ppermute(item, "req", pairs)

    *packed, own_tile = pack(0)
    first_moved = [send(item, shift) for item, shift in zip(packed, SHIFTS)]
    packed_last = pack(1)
    last_moved = []
    for item, ahead, shift in zip(packed_last, first_moved, SHIFTS):
        item, _ = lax.optimization_barrier((item, ahead))
        last_moved.append(send(item, shift))

    ids_rows, _ = lax.optimization_barrier((expert_ids.T, own_tile))
    spots, first, cand_out = pl.pallas_call(
        functools.partial(route_kernel, capacity),
        grid=(1,),
        in_specs=[
            whole(2, rows),
            whole(1, rows),
            pl.BlockSpec((rows, early), lambda i: (0, 0)),
        ],
        out_specs=[whole(8, 2 * rows), whole(rows, 128), whole(slots, early)],
        out_shape=[
            jax.ShapeDtypeStruct((8, 2 * rows), jnp.int32),
            jax.ShapeDtypeStruct((rows, 128), BF16),
            jax.ShapeDtypeStruct((slots, early), BF16),
        ],
        compiler_params=params(),
        cost_estimate=cost(5 * 10**8, 3 * 10**6),
        name="route",
    )(ids_rows, cand_request[None, :], cand_emb)

    def exchange(item):
        return lax.all_to_all(item, "exp", split_axis=0, concat_axis=0, tiled=True)

    cand_in = exchange(cand_out.reshape(experts, capacity, early))

    cand_rows, _, _ = lax.optimization_barrier((cand_emb, spots, packed_last[0]))
    steps = 4
    wide = 2 * feature // steps
    queries, update = pl.pallas_call(
        project_kernel,
        in_specs=[
            pl.BlockSpec(memory_space=pltpu.VMEM),
            anywhere,
            pl.BlockSpec(memory_space=pltpu.VMEM),
        ],
        out_shape=[
            jax.ShapeDtypeStruct((rows, feature), BF16),
            jax.ShapeDtypeStruct((rows, feature), F32),
        ],
        scratch_shapes=[pltpu.VMEM((steps, feature, wide), BF16), pltpu.SemaphoreType.DMA((steps,))],
        compiler_params=params(),
        cost_estimate=cost(11 * 10**8, 6 * 10**6, 2**18),
        name="project",
    )(cand_rows, w_query_update, norm_gain[None, :])

    hidden_count = w_up.shape[2]
    tile = 512
    def attend(chunk, moved, extra, out_shape, extra_scratch, name, flops):
        arrays = [queries, cache, *moved, *first_moved, own_tile, first, update, spots, *extra]
        out_rows = out_shape[0].shape
        parts = 2 * chunk_heads[chunk]
        wide = parts * 64
        return pl.pallas_call(
            functools.partial(attend_kernel, chunk),
            in_specs=[smem] * 3 + [anywhere] * len(arrays),
            out_specs=[anywhere] * len(out_shape),
            out_shape=out_shape,
            scratch_shapes=[
                pltpu.SemaphoreType.DMA((16 + 4 * parts,)),
                pltpu.VMEM((owners - 1, *moved[0].shape), BF16),
                pltpu.VMEM((2, keys, wide), BF16),
                pltpu.VMEM((owners, 16, 128), BF16),
                pltpu.VMEM((rows, wide), BF16),
                pltpu.VMEM((rows, 128), BF16),
                pltpu.VMEM((rows, wide), F32),
                pltpu.VMEM((8, 2 * rows), jnp.int32),
                pltpu.VMEM((slots, rows), BF16),
                pltpu.VMEM((rows, 128), F32),
                pltpu.VMEM((rows, wide), BF16),
                pltpu.VMEM(out_rows, BF16),
                *extra_scratch,
            ],
            compiler_params=params(),
            cost_estimate=cost(flops, 10**6),
            name=name,
        )(me_scalar, hist_blocks, rel_bias.T, *arrays)

    stuff_out, stuff, square = attend(
        0,
        first_moved,
        [],
        [
            jax.ShapeDtypeStruct((slots, early), BF16),
            jax.ShapeDtypeStruct((rows, early), BF16),
            jax.ShapeDtypeStruct((rows, 128), F32),
        ],
        [],
        "attend_first",
        FIRST_COST,
    )
    stuff_in = exchange(stuff_out.reshape(experts, capacity, early))

    tower_rows = jnp.pad(w_tower.T, ((0, 16 - tasks), (0, 0)))
    tower_rows, _ = lax.optimization_barrier((tower_rows, cand_in))
    towers = pl.pallas_call(
        tower_kernel,
        in_specs=[pl.BlockSpec(memory_space=pl.ANY), pl.BlockSpec(memory_space=pltpu.VMEM)],
        out_shape=jax.ShapeDtypeStruct((16, hidden_count), BF16),
        scratch_shapes=[
            pltpu.VMEM((hidden_count // tile, tile, feature), BF16),
            pltpu.SemaphoreType.DMA((hidden_count // tile,)),
        ],
        compiler_params=params(),
        cost_estimate=cost(10**8, 9 * 10**6),
        name="tower",
    )(w_down, tower_rows)


    square, _ = lax.optimization_barrier((square, towers))
    last_rows = chunk_heads[1] * capacity + 16
    late = feature - early
    last_out, late_mixed, row_scale = attend(
        1,
        last_moved,
        [cand_emb, square],
        [
            jax.ShapeDtypeStruct((experts, last_rows, 128), BF16),
            jax.ShapeDtypeStruct((rows, late), BF16),
            jax.ShapeDtypeStruct((rows, 128), F32),
        ],
        [pltpu.VMEM((rows, late), BF16), pltpu.VMEM((rows, late), F32)],
        "attend_last",
        LAST_COST,
    )
    last_in = exchange(last_out)
    wide = hidden_count // 4
    products = [jax.ShapeDtypeStruct((hidden_count, slots), BF16)] * 2
    cand_product, stuff_product = pl.pallas_call(
        early_kernel,
        in_specs=[anywhere] * 3,
        out_specs=[anywhere] * 2,
        out_shape=products,
        scratch_shapes=[
            pltpu.VMEM((2, experts, capacity, early), BF16),
            pltpu.VMEM((4, early, wide), BF16),
            pltpu.VMEM((2, early, slots), BF16),
            pltpu.VMEM((2, 4, wide, slots), BF16),
            pltpu.SemaphoreType.DMA((16,)),
        ],
        compiler_params=params(),
        cost_estimate=cost(EARLY_COST, 10**6),
        name="early",
    )(cand_in, stuff_in, w_up)

    gates = pl.pallas_call(
        functools.partial(gate_kernel, tasks),
        out_shape=jax.ShapeDtypeStruct((8, 2 * rows), F32),
        compiler_params=params(GATE_LIMIT),
        cost_estimate=cost(10**8, 2 * 10**6, 4096),
        name="gate",
    )(ids_rows, w_gate.T, cand_emb, stuff, late_mixed, row_scale)

    late = feature - early
    count = hidden_count // tile
    produced = pl.pallas_call(
        expert_kernel,
        in_specs=[anywhere] * 5,
        out_shape=jax.ShapeDtypeStruct((experts, 2, 128), F32),
        scratch_shapes=[
            pltpu.VMEM((experts, last_rows, 128), BF16),
            pltpu.VMEM((count, tile, slots), BF16),
            pltpu.VMEM((count, tile, slots), BF16),
            pltpu.VMEM((count, late, tile), BF16),
            pltpu.VMEM((16, hidden_count), BF16),
            pltpu.VMEM((late, slots), BF16),
            pltpu.VMEM((1, slots), F32),
            pltpu.SemaphoreType.DMA((3 * count + 2,)),
        ],
        compiler_params=params(),
        cost_estimate=cost(6 * 10**9, 25 * 10**6, 2**22),
        name="expert",
    )(last_in, cand_product, stuff_product, w_up, towers)

    came_back = exchange(produced)

    vmem = pl.BlockSpec(memory_space=pltpu.VMEM)
    scores = pl.pallas_call(
        functools.partial(combine_kernel, capacity),
        in_specs=[vmem, vmem, vmem, vmem],
        out_shape=jax.ShapeDtypeStruct((tasks, rows), F32),
        compiler_params=params(COMBINE_LIMIT),
        cost_estimate=cost(10**8, 10**6),
        name="combine",
    )(spots, ids_rows, gates, came_back.reshape(experts * 2, 128))
    return scores.T


def solution(mesh):
    placed = (
        P(("req", "exp"), None),
        P(("req", "exp")),
        P(("req", "exp")),
        P(("req", "exp"), None, None),
        P(("req", "exp")),
        P(),
        P(),
        P(),
        P(),
        P(("req", "exp"), None),
        P("exp", None, None),
        P("exp", None, None),
        P(),
    )
    return jax.shard_map(
        local, mesh=mesh, in_specs=placed, out_specs=P(("req", "exp"), None), check_vma=False
    )
```

```python
import functools
import math

import jax
import jax.numpy as jnp
from jax import lax
from jax.experimental import pallas as pl
from jax.experimental.pallas import tpu as pltpu
from jax.sharding import PartitionSpec as P

EPSILON = 1e-05
F32 = jnp.float32
BF16 = jnp.bfloat16
NT = (((1,), (1,)), ((), ()))
TN = (((0,), (0,)), ((), ()))
SHIFTS = (1, 3, 2)
HEADS_FIRST = 4
GATE_LIMIT = 8
COMBINE_LIMIT = 8
AHEAD = 3
FIRST_COST = 30 * 10**9
EARLY_COST = 5 * 10**9
LAST_COST = 100 * 10**9


def pack_kernel(chunk, me_ref, ids_ref, cache_at, *refs):
    count = len(SHIFTS)
    packed, sems = refs[-2:]
    outs = refs[:-2]
    owners, keys, width = cache_at.shape
    parts = packed.shape[1] // keys
    heads = parts // 2
    first = chunk * (width // 256 - heads)
    me = me_ref[0]
    loads = []
    for n, shift in enumerate(SHIFTS):
        to = lax.rem(me + shift, owners)
        for part in range(parts):
            col = (first + part % heads) * 128 + (part // heads) * (width // 2)
            here = packed.at[n, pl.ds(part * keys, keys), :]
            load = pltpu.make_async_copy(cache_at.at[to, :, pl.ds(col, 128)], here, sems.at[0, n, part])
            load.start()
            store = pltpu.make_async_copy(here, outs[n].at[pl.ds(part * keys, keys), :], sems.at[1, n, part])
            loads.append((load, store))
    stores = []
    if len(outs) > count:
        row = lax.broadcasted_iota(jnp.int32, (16, 128), 0)

        def tile_of(owner):
            one = ids_ref[2 * owner].astype(F32)
            two = ids_ref[2 * owner + 1].astype(F32)
            return jnp.where(row == 0, one, two).astype(BF16)

        for n, shift in enumerate(SHIFTS):
            here = pl.ds(parts * keys, 16)
            packed[n, here, :] = tile_of(lax.rem(me + shift, owners))
            store = pltpu.make_async_copy(packed.at[n, here, :], outs[n].at[here, :], sems.at[1, n, parts])
            store.start()
            stores.append(store)
        outs[count][...] = tile_of(me)
    for load, store in loads:
        load.wait()
        store.start()
        stores.append(store)
    for store in stores:
        store.wait()


def place_of(slot, slots):
    rows = slot.shape[1] // 2
    spot = lax.broadcasted_iota(jnp.int32, (slots, rows), 0)
    place = (spot == slot[:, :rows]) | (spot == slot[:, rows:])
    return jnp.where(place, 1.0, 0.0).astype(BF16)


def route_kernel(capacity, ids_ref, req_ref, cand_ref, spot_ref, first_ref, out_ref):
    rows = ids_ref.shape[1]
    experts = out_ref.shape[0] // capacity
    ids = jnp.concatenate([ids_ref[0:1, :], ids_ref[1:2, :]], axis=1)
    hot = lax.broadcasted_iota(jnp.int32, (experts, 2 * rows), 0) == ids
    hot = jnp.where(hot, 1.0, 0.0)
    here = lax.broadcasted_iota(jnp.int32, (2 * rows, 2 * rows), 0)
    there = lax.broadcasted_iota(jnp.int32, (2 * rows, 2 * rows), 1)
    earlier = jnp.where(here < there, 1.0, 0.0).astype(BF16)
    counts = jnp.dot(hot.astype(BF16), earlier, preferred_element_type=F32)
    position = jnp.sum(counts * hot, axis=0, keepdims=True).astype(jnp.int32)
    slot = ids * capacity + position
    spot_ref[...] = jnp.broadcast_to(slot, spot_ref.shape)
    place = place_of(slot, out_ref.shape[0])
    out_ref[...] = jnp.dot(place, cand_ref[...], preferred_element_type=F32).astype(BF16)
    first = jnp.where(req_ref[...] == 0, 1.0, 0.0)
    first_ref[...] = jnp.transpose(jnp.broadcast_to(first, (128, rows))).astype(BF16)


def project_kernel(cand_ref, weight_at, gain_ref, query_ref, update_ref, weight, sems):
    count, _, wide = weight.shape
    loads = []
    for i in range(count):
        here = pl.ds(i * wide, wide)
        loads.append(pltpu.make_async_copy(weight_at.at[:, here], weight.at[i], sems.at[i]))
        loads[i].start()
    for i in range(count):
        loads[i].wait()
        projected = jnp.dot(cand_ref[...], weight[i], preferred_element_type=F32)
        cols = pl.ds(i % (count // 2) * wide, wide)
        if i < count // 2:
            query_ref[:, cols] = projected.astype(BF16)
        else:
            update_ref[:, cols] = gain_ref[:, cols] * projected / (1.0 + jnp.exp(-projected))


def tower_kernel(down_at, tower_ref, out_ref, down, sems):
    count, tile, _ = down.shape
    feature = tower_ref.shape[1]
    weight = tower_ref[...].astype(F32)
    weight = jnp.concatenate([weight, jnp.zeros((16 - weight.shape[0], feature), F32)], axis=0)
    weight = weight.astype(BF16)
    loads = []
    for i in range(count):
        here = pl.ds(i * tile, tile)
        loads.append(pltpu.make_async_copy(down_at.at[0, here, :], down.at[i], sems.at[i]))
    for i in range(2):
        loads[i].start()
    for i in range(count):
        if i + 2 < count:
            loads[i + 2].start()
        loads[i].wait()
        product = lax.dot_general(weight, down[i], NT, preferred_element_type=F32)
        high = product.astype(BF16)
        low = (product - high.astype(F32)).astype(BF16)
        out_ref[:, pl.ds(i * tile, tile)] = jnp.concatenate([high[0:8], low[0:8]], axis=0)


def attend_head(head, first, mask, query, key, value, blocks, bias_ref):
    scores = lax.dot_general(query, key, NT, preferred_element_type=F32)
    weights = []
    for owner, (block_a, block_b) in enumerate(blocks):
        here = scores[:, owner * 256 : (owner + 1) * 256]
        here = jnp.where(first, here[:, :128], here[:, 128:])
        bias_a = jnp.zeros_like(block_a)
        bias_b = jnp.zeros_like(block_b)
        for block in range(bias_ref.shape[0]):
            entry = bias_ref[block, head] * 0.5
            bias_a = jnp.where(block_a == block, entry, bias_a)
            bias_b = jnp.where(block_b == block, entry, bias_b)
        half = here * (0.5 / math.sqrt(128.0)) + jnp.where(first, bias_a, bias_b)
        weight = (half + half * jnp.tanh(half)).astype(BF16)
        weights += [weight, weight]
    weights = jnp.concatenate(weights, axis=1) * mask
    return jnp.dot(weights, value, preferred_element_type=F32)


def attend_kernel(chunk, me_ref, hist_ref, bias_ref, *refs):
    last = chunk == 1
    query_at, cache_at, *refs = refs
    moved_at, refs = refs[:3], refs[3:]
    ids_at, refs = refs[:3], refs[3:]
    own_at, first_at, update_at, spot_at, *refs = refs
    if last:
        cand_at, square_at, *refs = refs
        out_at, mixed_at, scale_at, *refs = refs
    else:
        out_at, stuff_at, square_at, *refs = refs
    sems, kv, own, tiles, query, first_in, update, spot, place, square, stuff, out, *refs = refs
    if last:
        cand, attended = refs
    owners, keys, width = cache_at.shape
    heads = own.shape[2] // 128
    early = heads * 128
    base = chunk * (width // 256 - heads)
    id_row = ids_at[0].shape[0] - 16
    rows = query.shape[0]
    me = me_ref[0]
    used = []

    def copy(source, target):
        item = pltpu.make_async_copy(source, target, sems.at[len(used)])
        item.start()
        used.append(item)
        return item

    wanted = [copy(query_at.at[:, pl.ds(base * 128, early)], query)]
    wanted.append(copy(first_at, first_in))
    wanted.append(copy(own_at, tiles.at[0]))
    wanted.append(copy(spot_at, spot))
    if last:
        for n in range(3):
            wanted.append(copy(ids_at[n].at[pl.ds(id_row, 16), :], tiles.at[n + 1]))
    loads = [[copy(moved_at[n], kv.at[n])] for n in range(3)]
    for half in range(2):
        here = pl.ds(half * (width // 2) + base * 128, early)
        loads.append([copy(cache_at.at[me, :, here], own.at[half])])
    later = [copy(update_at.at[:, pl.ds(base * 128, early)], update)]
    if last:
        later += [copy(cand_at.at[:, pl.ds(base * 128, early)], cand), copy(square_at, square)]
    for item in wanted:
        item.wait()
    if not last:
        for n in range(3):
            loads[n][0].wait()
            tiles[n + 1] = kv[n, pl.ds(id_row, 16), :]
        loads = loads[3:]
    first = first_in[...].astype(F32) > 0.5
    length_a = hist_ref[0].astype(F32)
    length_b = hist_ref[1].astype(F32)
    blocks = []
    masks = []
    for owner in range(owners):
        tile = tiles[owner].astype(F32)
        block_a, block_b = tile[0:1, :], tile[1:2, :]
        blocks.append((block_a, block_b))
        mask_a = jnp.where(first, jnp.where(block_a < length_a, 1.0, 0.0), 0.0)
        mask_b = jnp.where(first, 0.0, jnp.where(block_b < length_b, 1.0, 0.0))
        masks += [mask_a.astype(BF16), mask_b.astype(BF16)]
    mask = jnp.concatenate(masks, axis=1)
    place[...] = place_of(spot[0:1, :], place.shape[0])
    total = None
    stores = []
    for load in loads:
        for item in load:
            item.wait()
    for item in later:
        item.wait()
    for head in range(heads):
        cols = pl.ds(head * 128, 128)
        at_key, at_value = pl.ds(head * keys, keys), pl.ds((heads + head) * keys, keys)
        key = jnp.concatenate([own[0, :, cols]] + [kv[n, at_key, :] for n in range(3)], axis=0)
        value = jnp.concatenate([own[1, :, cols]] + [kv[n, at_value, :] for n in range(3)], axis=0)
        found = attend_head(base + head, first, mask, query[:, cols], key, value, blocks, bias_ref)
        total = found * found if total is None else total + found * found
        if last:
            attended[:, cols] = found * update[:, cols]
            continue
        stuff[:, cols] = (found * update[:, cols]).astype(BF16)
        if head % 2 == 1 or head == heads - 1:
            here = pl.ds(head // 2 * 256, 256 if head % 2 else 128)
            out[:, here] = jnp.dot(place[...], stuff[:, here], preferred_element_type=F32).astype(BF16)
            stores.append(copy(out.at[:, here], out_at.at[:, here]))
    if not last:
        square[...] = total
        stores.append(copy(stuff, stuff_at))
        stores.append(copy(square, square_at))
        for item in stores:
            item.wait()
        return
    feature = width // 2
    mean = jnp.sum(total + square[...], axis=1, keepdims=True) * (1.0 / feature)
    inv_rms = lax.rsqrt(mean + EPSILON)
    peers = out.shape[0]
    share = place.shape[0] // peers
    for i in range((heads + 1) // 2):
        some = min(2, heads - 2 * i)
        cols = pl.ds(i * 256, some * 128)
        block = (cand[:, cols].astype(F32) + attended[:, cols] * inv_rms).astype(BF16)
        stuff[:, cols] = block
        sent = jnp.dot(place[...], block, preferred_element_type=F32).astype(BF16)
        for j in range(some):
            here = pl.ds((2 * i + j) * share, share)
            out[:, here, :] = sent[:, j * 128 : (j + 1) * 128].reshape(peers, share, 128)
    scale = jnp.transpose(jnp.broadcast_to(inv_rms, (rows, 128)))[0:16, :]
    high = scale.astype(BF16).astype(F32)
    row = lax.broadcasted_iota(jnp.int32, scale.shape, 0)
    scale = jnp.where(row == 0, high, jnp.where(row == 1, scale - high, 0.0)).astype(BF16)
    scale = lax.dot_general(scale, place[...], NT, preferred_element_type=F32)
    each = 128 // share
    for peer in range(peers):
        tile = scale[:, (peer // each) * 128 : (peer // each + 1) * 128]
        if peer % each:
            tile = pltpu.roll(tile, 128 - (peer % each) * share, 1)
        out[peer, pl.ds(heads * share, 16), :] = tile.astype(BF16)
    stores.append(copy(out, out_at))
    square[...] = jnp.broadcast_to(inv_rms, square.shape)
    stores.append(copy(stuff, mixed_at))
    stores.append(copy(square, scale_at))
    for item in stores:
        item.wait()


def gate_kernel(tasks, ids_ref, weight_ref, cand_ref, stuff_ref, late_ref, scale_ref, out_ref):
    rows, early = stuff_ref.shape
    experts = weight_ref.shape[0] // tasks
    mixed = cand_ref[:, :early].astype(F32) + stuff_ref[...].astype(F32) * scale_ref[:, 0:1]
    logits = lax.dot_general(weight_ref[:, :early], mixed.astype(BF16), NT, preferred_element_type=F32)
    logits += lax.dot_general(weight_ref[:, early:], late_ref[...], NT, preferred_element_type=F32)
    squashed = []
    for k in range(2):
        hot = lax.broadcasted_iota(jnp.int32, (experts, rows), 0) == ids_ref[k : k + 1, :]
        picked = []
        for task in range(8):
            if task < tasks:
                here = logits[task * experts : (task + 1) * experts, :]
                picked.append(jnp.sum(jnp.where(hot, here, 0.0), axis=0, keepdims=True))
            else:
                picked.append(jnp.zeros((1, rows), F32))
        squashed.append(jax.nn.sigmoid(jnp.concatenate(picked, axis=0)))
    whole = squashed[0] + squashed[1]
    for k in range(2):
        out_ref[:, pl.ds(k * rows, rows)] = squashed[k] / whole


def early_kernel(cand_at, stuff_at, up_at, cand_out_at, stuff_out_at, rows, up, turned, out, sems):
    _, peers, share, early = rows.shape
    count, _, tile = up.shape
    used = []

    def copy(source, target):
        item = pltpu.make_async_copy(source, target, sems.at[len(used)])
        used.append(item)
        return item

    fetch = [copy(cand_at, rows.at[0]), copy(stuff_at, rows.at[1])]
    ups = []
    for i in range(count):
        here = pl.ds(i * tile, tile)
        ups.append(copy(up_at.at[0, pl.ds(0, early), here], up.at[i]))
    fetch[0].start()
    ups[0].start()
    fetch[1].start()
    stores = []
    for k, out_at in enumerate((cand_out_at, stuff_out_at)):
        fetch[k].wait()
        for i in range(early // 128):
            cols = pl.ds(i * 128, 128)
            block = rows[k, :, :, cols].reshape(peers * share, 128)
            turned[k, cols, :] = jnp.transpose(block * jnp.asarray(0.5, BF16))
        for i in range(count):
            if k == 0:
                ups[i].wait()
                if i + 1 < count:
                    ups[i + 1].start()
            found = lax.dot_general(up[i], turned[k], TN, preferred_element_type=F32)
            out[k, i] = found.astype(BF16)
            store = copy(out.at[k, i], out_at.at[pl.ds(i * tile, tile), :])
            store.start()
            stores.append(store)
    for store in stores:
        store.wait()


def expert_kernel(
    last_at, cand_product_at, stuff_product_at, up_at, tower_at, out_ref,
    last, cand_product, stuff_product, up, tower, turned, scale, sems,
):
    count, late, tile = up.shape
    early = up_at.shape[1] - late
    peers = last.shape[0]
    share = (last.shape[1] - 16) // (late // 128)
    rows = peers * share
    each = 128 // share
    fetch = pltpu.make_async_copy(last_at, last, sems.at[0])
    fetch.start()
    fetch_tower = pltpu.make_async_copy(tower_at, tower, sems.at[1])
    fetch_tower.start()
    loads = []
    for i in range(count):
        here = pl.ds(i * tile, tile)
        loads.append(
            (
                pltpu.make_async_copy(up_at.at[0, pl.ds(early, late), here], up.at[i], sems.at[3 * i + 2]),
                pltpu.make_async_copy(cand_product_at.at[here, :], cand_product.at[i], sems.at[3 * i + 3]),
                pltpu.make_async_copy(stuff_product_at.at[here, :], stuff_product.at[i], sems.at[3 * i + 4]),
            )
        )
    for item in loads[0]:
        item.start()
    fetch.wait()
    for ahead in range(1, AHEAD):
        for item in loads[ahead]:
            item.start()
    lane = lax.broadcasted_iota(jnp.int32, (16, 128), 1)
    for group in range(peers // each):
        whole_tile = None
        for i in range(each):
            part = last[group * each + i, pl.ds(late // 128 * share, 16), :].astype(F32)
            part = pltpu.roll(part, i * share, 1) if i else part
            part = jnp.where((lane >= i * share) & (lane < (i + 1) * share), part, 0.0)
            whole_tile = part if whole_tile is None else whole_tile + part
        scale[:, pl.ds(group * 128, 128)] = whole_tile[0:1, :] + whole_tile[1:2, :]
    for i in range(late // 128):
        block = last[:, pl.ds(i * share, share), :].reshape(rows, 128)
        turned[pl.ds(i * 128, 128), :] = jnp.transpose(block * jnp.asarray(0.5, BF16))
    fetch_tower.wait()
    total = None
    row_scale = scale[...].astype(BF16)
    for i in range(count):
        if i + AHEAD < count:
            for item in loads[i + AHEAD]:
                item.start()
        for item in loads[i]:
            item.wait()
        half = lax.dot_general(up[i], turned[...], TN, preferred_element_type=F32)
        half = half + (cand_product[i] + stuff_product[i] * row_scale).astype(F32)
        hidden = (half + half * jnp.tanh(half)).astype(BF16)
        part = jnp.dot(tower[:, pl.ds(i * tile, tile)], hidden, preferred_element_type=F32)
        total = part if total is None else total + part
    found = total[0:8, :] + total[8:16, :]
    row = lax.broadcasted_iota(jnp.int32, (8, 128), 0)
    mine = lax.broadcasted_iota(jnp.int32, (8, 128), 1) // share == row % each
    for group in range(peers // each):
        tile = found[:, group * 128 : (group + 1) * 128]
        turns = [tile] + [pltpu.roll(tile, k * share, 1) for k in range(1, each)]
        for i in range(each):
            kept = jnp.zeros((8, 128), F32)
            for k in range(each):
                kept = jnp.where(mine & (row % each == (i + k) % each), turns[k], kept)
            rows_out = []
            for half in range(2):
                line = kept[half * 4 : half * 4 + 1]
                for j in range(1, 4):
                    line = line + kept[half * 4 + j : half * 4 + j + 1]
                rows_out.append(line)
            out_ref[group * each + i] = jnp.concatenate(rows_out, axis=0)


def combine_kernel(capacity, spot_ref, ids_ref, gate_ref, back_ref, out_ref):
    rows = ids_ref.shape[1]
    experts = back_ref.shape[0] // 2
    ids = jnp.concatenate([ids_ref[0:1, :], ids_ref[1:2, :]], axis=1)
    position = spot_ref[0:1, :] - ids * capacity
    back = back_ref[...]
    high = back.astype(BF16)
    rest = back - high.astype(F32)
    middle = rest.astype(BF16)
    low = (rest - middle.astype(F32)).astype(BF16)
    lanes = lax.broadcasted_iota(jnp.int32, (128, 2 * rows), 0)
    picked = []
    for task in range(128 // capacity):
        hot = jnp.where(lanes == position + task * capacity, 1.0, 0.0).astype(BF16)
        found = jnp.dot(high, hot, preferred_element_type=F32)
        found += jnp.dot(middle, hot, preferred_element_type=F32)
        found += jnp.dot(low, hot, preferred_element_type=F32)
        total = jnp.zeros((8, 2 * rows), F32)
        for group in range(experts // 4):
            owner = group * 4 + lax.broadcasted_iota(jnp.int32, (8, 2 * rows), 0) // 2
            total = total + jnp.where(ids == owner, found[group * 8 : (group + 1) * 8], 0.0)
        picked.append(total)
    lines = []
    for half in range(2):
        for total in picked:
            line = total[half : half + 1]
            for pair in range(1, 4):
                line = line + total[2 * pair + half : 2 * pair + half + 1]
            lines.append(line)
    total = jnp.concatenate(lines, axis=0) * gate_ref[...]
    total = total[:, :rows] + total[:, rows:]
    out_ref[...] = total[: out_ref.shape[0]]


def params(mib=63):
    return pltpu.CompilerParams(vmem_limit_bytes=mib * 2**20)


def cost(flops, bytes_accessed, transcendentals=0):
    return pl.CostEstimate(flops=flops, bytes_accessed=bytes_accessed, transcendentals=transcendentals)


def whole(*shape):
    return pl.BlockSpec(shape, lambda i, *_: (0,) * len(shape))


def local(
    cand_emb,
    cand_request,
    hist_blocks,
    cache_kv,
    block_map,
    w_query_update,
    rel_bias,
    norm_gain,
    w_gate,
    expert_ids,
    w_up,
    w_down,
    w_tower,
):
    rows, feature = cand_emb.shape
    owners = lax.axis_size("req")
    me = lax.axis_index("req").astype(jnp.int32)
    head_count = rel_bias.shape[0]
    tasks = w_tower.shape[1]
    experts = w_gate.shape[1] // tasks
    capacity = 2 * rows * expert_ids.shape[1] // experts
    slots = experts * capacity
    chunk_heads = (HEADS_FIRST, head_count - HEADS_FIRST)
    early = HEADS_FIRST * 128
    keys = cache_kv.shape[0] // owners * cache_kv.shape[1]
    me_scalar = me[None]
    smem = pl.BlockSpec(memory_space=pltpu.SMEM)
    anywhere = pl.BlockSpec(memory_space=pl.ANY)
    hbm = pl.BlockSpec(memory_space=pltpu.HBM)

    cache = cache_kv.reshape(owners, keys, 2 * feature)

    def pack(chunk):
        parts = 2 * chunk_heads[chunk]
        tail = 16 if chunk == 0 else 0
        shapes = [jax.ShapeDtypeStruct((parts * keys + tail, 128), BF16)] * len(SHIFTS)
        specs = [anywhere] * len(SHIFTS)
        if chunk == 0:
            shapes.append(jax.ShapeDtypeStruct((16, 128), BF16))
            specs.append(pl.BlockSpec(memory_space=pltpu.VMEM))
        return pl.pallas_call(
            functools.partial(pack_kernel, chunk),
            in_specs=[smem, smem, anywhere],
            out_specs=specs,
            out_shape=shapes,
            scratch_shapes=[
                pltpu.VMEM((len(SHIFTS), parts * keys + tail, 128), BF16),
                pltpu.SemaphoreType.DMA((2, len(SHIFTS), parts + 1)),
            ],
            compiler_params=params(),
            cost_estimate=cost(0, 10**6),
            name="pack",
        )(me_scalar, block_map, cache)

    def send(item, shift):
        pairs = [(i, (i + shift) % owners) for i in range(owners)]
        return lax.ppermute(item, "req", pairs)

    *packed, own_tile = pack(0)
    first_moved = [send(item, shift) for item, shift in zip(packed, SHIFTS)]
    packed_last = pack(1)
    last_moved = []
    for item, ahead, shift in zip(packed_last, first_moved, SHIFTS):
        item, _ = lax.optimization_barrier((item, ahead))
        last_moved.append(send(item, shift))

    ids_rows, _ = lax.optimization_barrier((expert_ids.T, own_tile))
    spots, first, cand_out = pl.pallas_call(
        functools.partial(route_kernel, capacity),
        grid=(1,),
        in_specs=[
            whole(2, rows),
            whole(1, rows),
            pl.BlockSpec((rows, early), lambda i: (0, 0)),
        ],
        out_specs=[whole(8, 2 * rows), whole(rows, 128), whole(slots, early)],
        out_shape=[
            jax.ShapeDtypeStruct((8, 2 * rows), jnp.int32),
            jax.ShapeDtypeStruct((rows, 128), BF16),
            jax.ShapeDtypeStruct((slots, early), BF16),
        ],
        compiler_params=params(),
        cost_estimate=cost(5 * 10**8, 3 * 10**6),
        name="route",
    )(ids_rows, cand_request[None, :], cand_emb)

    def exchange(item):
        return lax.all_to_all(item, "exp", split_axis=0, concat_axis=0, tiled=True)

    cand_in = exchange(cand_out.reshape(experts, capacity, early))

    cand_rows, _, _ = lax.optimization_barrier((cand_emb, spots, packed_last[0]))
    steps = 4
    wide = 2 * feature // steps
    queries, update = pl.pallas_call(
        project_kernel,
        in_specs=[
            pl.BlockSpec(memory_space=pltpu.VMEM),
            anywhere,
            pl.BlockSpec(memory_space=pltpu.VMEM),
        ],
        out_shape=[
            jax.ShapeDtypeStruct((rows, feature), BF16),
            jax.ShapeDtypeStruct((rows, feature), F32),
        ],
        scratch_shapes=[pltpu.VMEM((steps, feature, wide), BF16), pltpu.SemaphoreType.DMA((steps,))],
        compiler_params=params(),
        cost_estimate=cost(11 * 10**8, 6 * 10**6, 2**18),
        name="project",
    )(cand_rows, w_query_update, norm_gain[None, :])

    hidden_count = w_up.shape[2]
    tile = 512
    def attend(chunk, moved, extra, out_shape, extra_scratch, name, flops):
        arrays = [queries, cache, *moved, *first_moved, own_tile, first, update, spots, *extra]
        out_rows = out_shape[0].shape
        parts = 2 * chunk_heads[chunk]
        wide = parts * 64
        return pl.pallas_call(
            functools.partial(attend_kernel, chunk),
            in_specs=[smem] * 3 + [anywhere] * len(arrays),
            out_specs=[anywhere] * len(out_shape),
            out_shape=out_shape,
            scratch_shapes=[
                pltpu.SemaphoreType.DMA((16 + 4 * parts,)),
                pltpu.VMEM((owners - 1, *moved[0].shape), BF16),
                pltpu.VMEM((2, keys, wide), BF16),
                pltpu.VMEM((owners, 16, 128), BF16),
                pltpu.VMEM((rows, wide), BF16),
                pltpu.VMEM((rows, 128), BF16),
                pltpu.VMEM((rows, wide), F32),
                pltpu.VMEM((8, 2 * rows), jnp.int32),
                pltpu.VMEM((slots, rows), BF16),
                pltpu.VMEM((rows, 128), F32),
                pltpu.VMEM((rows, wide), BF16),
                pltpu.VMEM(out_rows, BF16),
                *extra_scratch,
            ],
            compiler_params=params(),
            cost_estimate=cost(flops, 10**6),
            name=name,
        )(me_scalar, hist_blocks, rel_bias.T, *arrays)

    stuff_out, stuff, square = attend(
        0,
        first_moved,
        [],
        [
            jax.ShapeDtypeStruct((slots, early), BF16),
            jax.ShapeDtypeStruct((rows, early), BF16),
            jax.ShapeDtypeStruct((rows, 128), F32),
        ],
        [],
        "attend_first",
        FIRST_COST,
    )
    stuff_in = exchange(stuff_out.reshape(experts, capacity, early))

    tower_rows, _ = lax.optimization_barrier((w_tower.T, cand_in))
    towers = pl.pallas_call(
        tower_kernel,
        in_specs=[pl.BlockSpec(memory_space=pl.ANY), pl.BlockSpec(memory_space=pltpu.VMEM)],
        out_shape=jax.ShapeDtypeStruct((16, hidden_count), BF16),
        scratch_shapes=[
            pltpu.VMEM((hidden_count // tile, tile, feature), BF16),
            pltpu.SemaphoreType.DMA((hidden_count // tile,)),
        ],
        compiler_params=params(),
        cost_estimate=cost(10**8, 9 * 10**6),
        name="tower",
    )(w_down, tower_rows)


    square, _ = lax.optimization_barrier((square, towers))
    last_rows = chunk_heads[1] * capacity + 16
    late = feature - early
    last_out, late_mixed, row_scale = attend(
        1,
        last_moved,
        [cand_emb, square],
        [
            jax.ShapeDtypeStruct((experts, last_rows, 128), BF16),
            jax.ShapeDtypeStruct((rows, late), BF16),
            jax.ShapeDtypeStruct((rows, 128), F32),
        ],
        [pltpu.VMEM((rows, late), BF16), pltpu.VMEM((rows, late), F32)],
        "attend_last",
        LAST_COST,
    )
    last_in = exchange(last_out)
    wide = hidden_count // 4
    products = [jax.ShapeDtypeStruct((hidden_count, slots), BF16)] * 2
    cand_product, stuff_product = pl.pallas_call(
        early_kernel,
        in_specs=[anywhere] * 3,
        out_specs=[anywhere] * 2,
        out_shape=products,
        scratch_shapes=[
            pltpu.VMEM((2, experts, capacity, early), BF16),
            pltpu.VMEM((4, early, wide), BF16),
            pltpu.VMEM((2, early, slots), BF16),
            pltpu.VMEM((2, 4, wide, slots), BF16),
            pltpu.SemaphoreType.DMA((16,)),
        ],
        compiler_params=params(),
        cost_estimate=cost(EARLY_COST, 10**6),
        name="early",
    )(cand_in, stuff_in, w_up)

    gates = pl.pallas_call(
        functools.partial(gate_kernel, tasks),
        out_shape=jax.ShapeDtypeStruct((8, 2 * rows), F32),
        compiler_params=params(GATE_LIMIT),
        cost_estimate=cost(10**8, 2 * 10**6, 4096),
        name="gate",
    )(ids_rows, w_gate.T, cand_emb, stuff, late_mixed, row_scale)

    late = feature - early
    count = hidden_count // tile
    produced = pl.pallas_call(
        expert_kernel,
        in_specs=[anywhere] * 5,
        out_shape=jax.ShapeDtypeStruct((experts, 2, 128), F32),
        scratch_shapes=[
            pltpu.VMEM((experts, last_rows, 128), BF16),
            pltpu.VMEM((count, tile, slots), BF16),
            pltpu.VMEM((count, tile, slots), BF16),
            pltpu.VMEM((count, late, tile), BF16),
            pltpu.VMEM((16, hidden_count), BF16),
            pltpu.VMEM((late, slots), BF16),
            pltpu.VMEM((1, slots), F32),
            pltpu.SemaphoreType.DMA((3 * count + 2,)),
        ],
        compiler_params=params(),
        cost_estimate=cost(6 * 10**9, 25 * 10**6, 2**22),
        name="expert",
    )(last_in, cand_product, stuff_product, w_up, towers)

    came_back = exchange(produced)

    vmem = pl.BlockSpec(memory_space=pltpu.VMEM)
    scores = pl.pallas_call(
        functools.partial(combine_kernel, capacity),
        in_specs=[vmem, vmem, vmem, vmem],
        out_shape=jax.ShapeDtypeStruct((tasks, rows), F32),
        compiler_params=params(COMBINE_LIMIT),
        cost_estimate=cost(10**8, 10**6),
        name="combine",
    )(spots, ids_rows, gates, came_back.reshape(experts * 2, 128))
    return scores.T


def solution(mesh):
    placed = (
        P(("req", "exp"), None),
        P(("req", "exp")),
        P(("req", "exp")),
        P(("req", "exp"), None, None),
        P(("req", "exp")),
        P(),
        P(),
        P(),
        P(),
        P(("req", "exp"), None),
        P("exp", None, None),
        P("exp", None, None),
        P(),
    )
    return jax.shard_map(
        local, mesh=mesh, in_specs=placed, out_specs=P(("req", "exp"), None), check_vma=False
    )
```
